256 devices in a mesh: section: 4 (over y), expert: 8 (over z_hi, core), dp: 8 (over z_lo, x).
Axes of the slice: x: 4, y: 4, z: 8 (z_hi: 4, z_lo: 2; z = z_hi * 2 + z_lo), core: 2. Of those that a mesh axis runs over, the one named last changes fastest.
Arguments:
- layer_input: bfloat16 [4096, 2048], P(('section', 'expert')), may hold values from -6 to 6
- out_grad: bfloat16 [4096, 2048], P(('section', 'expert')), may hold values from -6 to 6
- expert_ids: int32 [4096, 2], P(('section', 'expert')), may hold values from 0 to 3, all different within a row; in each aligned block of 128 rows (0 to 127, 128 to 255, ...) at most 80 rows name the same one
- gate_weights: bfloat16 [4096, 2], P(('section', 'expert')), may hold values from 0.01 to 0.99, as said below
- w_gate: bfloat16 [4, 32768, 2048], P('section', ('expert', 'dp')), may hold values from -0.125 to 0.125
- w_up: bfloat16 [4, 32768, 2048], P('section', ('expert', 'dp')), may hold values from -0.125 to 0.125
- w_down: bfloat16 [4, 32768, 2048], P('section', ('expert', 'dp')), may hold values from -0.0625 to 0.0625
Outputs:
- prev_grad: bfloat16 [4096, 2048], P(('section', 'expert'))
- router_grad: float32 [4096, 2], P(('section', 'expert'))
- grad_gate: bfloat16 [4, 32768, 2048], P('section', ('expert', 'dp'))
- grad_up: bfloat16 [4, 32768, 2048], P('section', ('expert', 'dp'))
- grad_down: bfloat16 [4, 32768, 2048], P('section', ('expert', 'dp'))
The draws below stay inside these ranges and needn't reach their ends.
Inputs may be any that keep to these rules, and one draw needn't show every extreme that they name: `expert_ids`: A token names 2 different experts. In each aligned block of 128 rows (the tokens of one device) no expert is named by more than 80 tokens. `gate_weights`: A token's two gate weights sum to one up to rounding; the first is no smaller than the second.
All inputs are finite; a program needn't handle non-finite values.
Results may differ from the reference program's by a relative error of at most 0.0049.
Values may be sent and summed in bfloat16 or wider, within the bound.
No kernel may reach another device: no remote copies, remote signals or barrier semaphores. Data moves between devices by JAX's collectives and lax.ppermute only.
A program may use at most 128 MiB of HBM per device.

```python
import math
import jax
import jax.numpy as jnp
import numpy as np

D = 2048
FF = 8192
EXPERTS = 4
TOP = 2
TOK_DEV = 128
CAP = 80
LAYERS = 4
SECTION_TOKENS = 1024
TOKENS = 4096
UNITS = 32768


def draw_gate_weights(key, part):
    first = jax.random.uniform(key, (TOKENS, 1), jnp.float32, 0.5, 0.99)
    return jnp.concatenate([first, 1.0 - first], axis=1).astype(jnp.bfloat16)


def level_of(stream_key, dims, split, least, high):
    level, own = 1.0, jax.random.fold_in(stream_key, 6)
    for axis_at, blocks in split:
        heights = jnp.exp(jax.random.uniform(jax.random.fold_in(own, axis_at), (blocks,), jnp.float32, least / len(split), high / len(split)))
        level = level * jnp.repeat(heights, dims[axis_at] // blocks).reshape([-1 if axis == axis_at else 1 for axis in range(len(dims))])
    return level


def shared_out(stream_key, own, number, rows, count, top, limit, lean):
    sequence = jax.random.permutation(stream_key, count)
    heavy_load, common = portions_of(count, rows * top, limit, lean, True), portions_of(count, rows * top, limit, lean, False)
    places = jnp.arange(count)

    def named(tallies, rotation):
        used = int((tallies > 0).sum())
        fixed = max(1, used // 4)
        moved = fixed + (places - fixed + rotation * (used - fixed)) % max(1, count - fixed)
        return jnp.zeros((count,), jnp.int32).at[sequence[jnp.where(places < fixed, places, moved)]].set(jnp.asarray(tallies, jnp.int32))

    tallies = jnp.where(number % 4 == 0, named(heavy_load, number // 4), named(common, number - number // 4 - 1))
    mixed = jax.random.permutation(jax.random.fold_in(own, 3), count)
    giver, sink = mixed[0:count // 2 * 2:2], mixed[1:count // 2 * 2:2]
    slack = jnp.minimum(tallies[giver] - 1, limit - tallies[sink]) // 2
    slack = jnp.where((giver == sequence[0]) | (sink == sequence[0]) | (tallies[sink] == 0), 0, jnp.maximum(slack, 0))
    moved = jax.random.randint(jax.random.fold_in(own, 4), (count // 2,), 0, 1 << 20) % (slack + 1)
    tallies = tallies.at[giver].add(-moved).at[sink].add(moved)
    labels = jnp.searchsorted(jnp.cumsum(tallies), jnp.arange(rows * top), side="right").astype(jnp.int32)
    listing = labels.reshape(top, rows).T
    listing = listing[jax.random.permutation(jax.random.fold_in(own, 1), rows)]
    rotation = jax.random.randint(jax.random.fold_in(own, 2), (rows, 1), 0, top)
    return jnp.take_along_axis(listing, (jnp.arange(top)[None, :] + rotation) % top, axis=1)


def portions_of(amount, total, reach, skew, full):
    weights = [(1 << 20) // math.isqrt(grade ** skew) + 1 for grade in range(1, amount + 1)]
    largest = reach if full else min(reach, max(-(-total // amount), total * weights[0] // sum(weights)))
    least = 1 if total - largest >= amount - 1 else 0
    counts, rest = [largest] + [least] * (amount - 1), total - largest - least * (amount - 1)
    while rest > 0:
        free = [i for i in range(1, amount) if counts[i] < largest] or [i for i in range(1, amount) if counts[i] < reach]
        whole, budget = sum([weights[i] for i in free]), rest
        for i in free:
            addition = min(reach - counts[i], max(1, budget * weights[i] // whole), rest)
            counts[i] = counts[i] + addition
            rest = rest - addition
    return np.array(counts)


def bell_draw(stream_key, dims, scale, limit, pieces=(), held_as=jnp.bfloat16):
    array = jax.random.normal(stream_key, dims, jnp.float32) * scale
    if len(pieces) > 0:
        array = level_of(stream_key, dims, pieces, -0.22, 0.18) * array
    return jnp.clip(array, min=-limit, max=limit).astype(held_as)


def setup_inputs(seed: int = 0) -> dict:
    streams_of = jax.random.split(jax.random.key(seed), 8)
    layer_input = bell_draw(streams_of[0], (TOKENS, D), 1.0, 6.0, ((0, 32),))
    out_grad = bell_draw(streams_of[1], (TOKENS, D), 1.0, 6.0, ((0, 32),))
    expert_ids_keys = jax.random.split(jax.random.fold_in(streams_of[2], 1), TOKENS // TOK_DEV)
    expert_ids_turns = jax.random.permutation(jax.random.fold_in(streams_of[2], 3), TOKENS // TOK_DEV)
    expert_ids = jax.vmap(lambda own, number: shared_out(jax.random.fold_in(streams_of[2], 2), own, number, TOK_DEV, EXPERTS, TOP, CAP, 2))(expert_ids_keys, expert_ids_turns).reshape((TOKENS, TOP))
    gate_weights = draw_gate_weights(jax.random.fold_in(streams_of[7], 71), 0)
    w_gate = bell_draw(streams_of[4], (LAYERS, UNITS, D), D ** -0.5, 0.125, ((0, 4), (1, 64)))
    w_up = bell_draw(streams_of[5], (LAYERS, UNITS, D), D ** -0.5, 0.125, ((0, 4), (1, 64)))
    w_down = bell_draw(streams_of[6], (LAYERS, UNITS, D), FF ** -0.5, 0.0625, ((0, 4), (1, 64)))
    return dict(layer_input=layer_input, out_grad=out_grad, expert_ids=expert_ids, gate_weights=gate_weights, w_gate=w_gate, w_up=w_up, w_down=w_down)


def expert_terms(inputs, grads_out, gates, expert_ids, gate_rows, up_rows, down_rows, expert):
    chosen = expert_ids == expert
    gate_share = jnp.sum(jnp.where(chosen, gates.astype(jnp.float32), jnp.float32(0.0)), axis=1)
    pre_gate = jnp.dot(inputs, gate_rows.T, preferred_element_type=jnp.float32)
    pre_up = jnp.dot(inputs, up_rows.T, preferred_element_type=jnp.float32)
    hidden_grad = jnp.dot(grads_out, down_rows.T, preferred_element_type=jnp.float32)
    sigmoid_gate = jax.nn.sigmoid(pre_gate)
    activated = pre_gate * sigmoid_gate
    hidden = activated * pre_up
    router_share = jnp.sum(hidden * hidden_grad, axis=1)
    scaled_grad = gate_share[:, None] * hidden_grad
    gate_pre_grad = (scaled_grad * pre_up * (sigmoid_gate * (1.0 + pre_gate * (1.0 - sigmoid_gate)))).astype(jnp.bfloat16)
    up_pre_grad = (scaled_grad * activated).astype(jnp.bfloat16)
    scaled_hidden = (gate_share[:, None] * hidden).astype(jnp.bfloat16)
    input_term = jnp.dot(gate_pre_grad, gate_rows, preferred_element_type=jnp.float32) + jnp.dot(up_pre_grad, up_rows, preferred_element_type=jnp.float32)
    gate_wgrad = jnp.dot(gate_pre_grad.T, inputs, preferred_element_type=jnp.float32).astype(jnp.bfloat16)
    up_wgrad = jnp.dot(up_pre_grad.T, inputs, preferred_element_type=jnp.float32).astype(jnp.bfloat16)
    down_wgrad = jnp.dot(scaled_hidden.T, grads_out, preferred_element_type=jnp.float32).astype(jnp.bfloat16)
    router_term = jnp.where(chosen, router_share[:, None], jnp.float32(0.0))
    return input_term, router_term, gate_wgrad, up_wgrad, down_wgrad


def reference(layer_input, out_grad, expert_ids, gate_weights, w_gate, w_up, w_down):
    input_blocks = []
    router_blocks = []
    gate_layers = []
    up_layers = []
    down_layers = []
    for section_index in range(LAYERS):
        first_row = section_index * SECTION_TOKENS
        inputs = layer_input[first_row:first_row + SECTION_TOKENS]
        grads_out = out_grad[first_row:first_row + SECTION_TOKENS]
        section_ids = expert_ids[first_row:first_row + SECTION_TOKENS]
        section_gates = gate_weights[first_row:first_row + SECTION_TOKENS]
        summed = grads_out.astype(jnp.float32)
        router = jnp.zeros((SECTION_TOKENS, TOP), jnp.float32)
        gate_parts = []
        up_parts = []
        down_parts = []
        for expert in range(EXPERTS):
            first_unit = expert * FF
            input_term, router_term, gate_wgrad, up_wgrad, down_wgrad = expert_terms(
                inputs, grads_out, section_gates, section_ids,
                w_gate[section_index, first_unit:first_unit + FF],
                w_up[section_index, first_unit:first_unit + FF],
                w_down[section_index, first_unit:first_unit + FF], expert)
            summed = summed + input_term
            router = router + router_term
            gate_parts.append(gate_wgrad)
            up_parts.append(up_wgrad)
            down_parts.append(down_wgrad)
        input_blocks.append(summed.astype(jnp.bfloat16))
        router_blocks.append(router)
        gate_layers.append(jnp.concatenate(gate_parts, axis=0))
        up_layers.append(jnp.concatenate(up_parts, axis=0))
        down_layers.append(jnp.concatenate(down_parts, axis=0))
    input_grad = jnp.concatenate(input_blocks, axis=0)
    prev_grad = jnp.roll(input_grad, -SECTION_TOKENS, axis=0)
    router_grad = jnp.concatenate(router_blocks, axis=0)
    return prev_grad, router_grad, jnp.stack(gate_layers), jnp.stack(up_layers), jnp.stack(down_layers)
```

```python
import jax
import jax.numpy as jnp
from jax import lax
from jax.experimental import pallas as pl
from jax.experimental.pallas import tpu as pltpu
from jax.sharding import PartitionSpec as P

EXPERTS = 4
CAP = 80
TOK = 128
D = 2048
UNITS = 512
ROWS = 640
PAIR = 2 * CAP
BF = jnp.bfloat16
F32 = jnp.float32
MIB = 1 << 20


def cost(flops, moved):
    return pl.CostEstimate(flops=flops, bytes_accessed=moved, transcendentals=0)


def core_swap(a):
    return lax.ppermute(a, "expert", [(i, i ^ 1) for i in range(8)])


def chip_shift(a, r):
    return lax.ppermute(a, "expert", [(i, (i + 2 * r) % 8) for i in range(8)])


def x_shift(a, j):
    return lax.ppermute(a, "dp", [(i, i // 4 * 4 + (i + j) % 4) for i in range(8)])


def pair_swap(a):
    return lax.ppermute(a, "dp", [(i, (i + 4) % 8) for i in range(8)])


def previous_section(a, flip):
    route = [(s * 8 + e, (s - 1) % 4 * 8 + (e ^ flip)) for s in range(4) for e in range(8)]
    return lax.ppermute(a, ("section", "expert"), route)


def dot(a, b, dims):
    return lax.dot_general(a, b, (dims, ((), ())), preferred_element_type=F32)


def slots_kernel(where_ref, mine_ref, got_ref, *outs):
    zin, zgr, routed_ref, og_ref = outs[:4], outs[4:8], outs[8], outs[9]
    core = where_ref[1]
    earlier = lax.broadcasted_iota(jnp.int32, (TOK, TOK), 0)
    later = lax.broadcasted_iota(jnp.int32, (TOK, TOK), 1)
    upto = (earlier <= later).astype(F32).astype(BF)
    slot = lax.broadcasted_iota(jnp.int32, (TOK, TOK), 0).astype(F32)
    row = lax.broadcasted_iota(jnp.int32, (16, TOK), 0)
    gate_rows = []
    for c in range(2):
        block = jnp.where(core == c, mine_ref[...].astype(F32), got_ref[...].astype(F32)).astype(BF)
        tokens = block[:TOK]
        meta = block[TOK : TOK + 16, :TOK]
        named = meta.astype(F32)
        place = dot(meta, upto, ((1,), (0,))) - 1.0
        og_ref[c] = tokens[:, 256:]
        for r in range(EXPERTS):
            hit = (slot == place[r : r + 1]) & (named[r : r + 1] > 0.5)
            hot = hit.astype(F32).astype(BF)
            routed_ref[c, r] = hot[:CAP]
            filled = dot(hot[:CAP], tokens, ((1,), (0,))).astype(BF)
            zin[r][c * CAP : (c + 1) * CAP, :] = filled[:, :256]
            zgr[r][c * CAP : (c + 1) * CAP, :] = filled[:, 256:]
            gates = dot(meta, hot, ((1,), (1,)))
            gate_rows.append(gates[4 + r : 5 + r])
    for r in range(EXPERTS):
        tile = jnp.where(row == 0, gate_rows[r], jnp.where(row == 1, gate_rows[4 + r], 0.0))
        zgr[r][PAIR : PAIR + 16, :TOK] = tile.astype(BF)
        zgr[r][PAIR : PAIR + 16, TOK:] = jnp.zeros((16, TOK), BF)


def fill_slots(where, mine, got):
    shapes = (
        [jax.ShapeDtypeStruct((PAIR, 256), BF)] * 4
        + [jax.ShapeDtypeStruct((PAIR + 16, 256), BF)] * 4
        + [
            jax.ShapeDtypeStruct((2, EXPERTS, CAP, TOK), BF),
            jax.ShapeDtypeStruct((2, TOK, 256), BF),
        ]
    )
    return pl.pallas_call(
        slots_kernel,
        out_shape=shapes,
        in_specs=[pl.BlockSpec(memory_space=pltpu.SMEM)]
        + [pl.BlockSpec(memory_space=pltpu.VMEM)] * 2,
        out_specs=[pl.BlockSpec(memory_space=pltpu.VMEM)] * 10,
        compiler_params=pltpu.CompilerParams(vmem_limit_bytes=8 * MIB),
        cost_estimate=cost(100_000_000, 2_000_000),
        name="fill_slots",
    )(where, mine, got)


def column(where_ref, j, flip):
    x, core = where_ref[0], where_ref[1]
    half = core if flip == 0 else 1 - core
    return pl.multiple_of(lax.rem(x + j, 4) * 512 + half * 256, 256)


def assemble(where_ref, pieces, whole):
    for flip in range(2):
        own, left, right, far_a, far_b = pieces[5 * flip : 5 * flip + 5]
        whole[:, pl.ds(column(where_ref, 0, flip), 256)] = own[...]
        whole[:, pl.ds(column(where_ref, 3, flip), 256)] = left[...]
        whole[:, pl.ds(column(where_ref, 1, flip), 256)] = right[...]
        whole[: ROWS // 2, pl.ds(column(where_ref, 2, flip), 256)] = far_a[...]
        whole[ROWS // 2 :, pl.ds(column(where_ref, 2, flip), 256)] = far_b[...]


def first_kernel(where_ref, *refs):
    pieces, (gate_ref, up_ref, whole, pre_gate, pre_up) = refs[:10], refs[10:]
    assemble(where_ref, pieces, whole)

    @pl.loop(0, 2)
    def _(n):
        units = pl.ds(pl.multiple_of(n * 256, 256), 256)
        pre_gate[:, units] = dot(whole[...], gate_ref[units, :], ((1,), (1,)))
        pre_up[:, units] = dot(whole[...], up_ref[units, :], ((1,), (1,)))


def first_work(where, pieces, w_gate, w_up):
    vmem = pl.BlockSpec(memory_space=pltpu.VMEM)
    return pl.pallas_call(
        first_kernel,
        out_shape=[
            jax.ShapeDtypeStruct((ROWS, D), BF),
            jax.ShapeDtypeStruct((ROWS, UNITS), F32),
            jax.ShapeDtypeStruct((ROWS, UNITS), F32),
        ],
        in_specs=[pl.BlockSpec(memory_space=pltpu.SMEM)] + [vmem] * 12,
        out_specs=[vmem] * 3,
        compiler_params=pltpu.CompilerParams(vmem_limit_bytes=24 * MIB),
        cost_estimate=cost(2 * 2 * ROWS * D * UNITS, 12_000_000),
        name="first_work",
    )(where, *pieces, w_gate, w_up)


def second_kernel(where_ref, *refs):
    pieces = refs[:10]
    down_ref, pre_gate, pre_up, gates_ref, gate_ref, up_ref = refs[10:16]
    whole, gpg, upg, scaled, router, keep, send = refs[16:]
    assemble(where_ref, pieces, whole)
    router[...] = jnp.zeros_like(router)

    @pl.loop(0, 2)
    def _(n):
        units = pl.ds(pl.multiple_of(n * 256, 256), 256)
        hidden_grad = dot(whole[...], down_ref[units, :], ((1,), (1,)))
        v = pre_gate[:, units]
        up = pre_up[:, units]
        gates = gates_ref[...]
        s = jax.nn.sigmoid(v)
        activated = v * s
        hidden = activated * up
        router[...] += jnp.sum(hidden * hidden_grad, axis=1, keepdims=True)
        scaled_grad = gates * hidden_grad
        gpg[:, units] = (scaled_grad * up * (s * (1.0 + v * (1.0 - s)))).astype(BF)
        upg[:, units] = (scaled_grad * activated).astype(BF)
        scaled[:, units] = (gates * hidden).astype(BF)

    @pl.loop(0, 4)
    def _(j):
        for flip in range(2):
            columns = pl.ds(column(where_ref, j, flip), 256)
            part = dot(gpg[...], gate_ref[:, columns], ((1,), (0,)))
            part = part + dot(upg[...], up_ref[:, columns], ((1,), (0,)))
            if flip == 0:
                keep[j] = part
            else:
                send[j] = part.astype(BF)


def second_work(where, pieces, w_down, pre_gate, pre_up, gates, w_gate, w_up):
    vmem = pl.BlockSpec(memory_space=pltpu.VMEM)
    return pl.pallas_call(
        second_kernel,
        out_shape=[
            jax.ShapeDtypeStruct((ROWS, D), BF),
            jax.ShapeDtypeStruct((ROWS, UNITS), BF),
            jax.ShapeDtypeStruct((ROWS, UNITS), BF),
            jax.ShapeDtypeStruct((ROWS, UNITS), BF),
            jax.ShapeDtypeStruct((ROWS, 1), F32),
            jax.ShapeDtypeStruct((4, ROWS, 256), F32),
            jax.ShapeDtypeStruct((4, ROWS, 256), BF),
        ],
        in_specs=[pl.BlockSpec(memory_space=pltpu.SMEM)] + [vmem] * 16,
        out_specs=[vmem] * 7,
        compiler_params=pltpu.CompilerParams(vmem_limit_bytes=40 * MIB),
        cost_estimate=cost(3 * 2 * ROWS * D * UNITS, 24_000_000),
        name="second_work",
    )(where, *pieces, w_down, pre_gate, pre_up, gates, w_gate, w_up)


def return_kernel(*refs):
    parts, (routed_ref, out_ref) = refs[:4], refs[4:]
    row = lax.broadcasted_iota(jnp.int32, (16, TOK), 0)
    router = jnp.zeros((16, TOK), F32)
    for c in range(2):
        total = jnp.zeros((TOK, 256), F32)
        for r in range(EXPERTS):
            hot = routed_ref[c, r]
            total += dot(hot, parts[r][c * CAP : (c + 1) * CAP, :], ((0,), (0,)))
            tail = dot(parts[r][PAIR : PAIR + 16, :CAP], hot, ((1,), (0,)))
            value = tail[2 * c : 2 * c + 1] + tail[2 * c + 1 : 2 * c + 2]
            router = jnp.where(row == 4 * c + r, value, router)
        out_ref[c * TOK : (c + 1) * TOK, :] = total
    out_ref[2 * TOK :, :TOK] = router
    out_ref[2 * TOK :, TOK:] = jnp.zeros((16, TOK), F32)


def return_slots(parts, routed):
    vmem = pl.BlockSpec(memory_space=pltpu.VMEM)
    return pl.pallas_call(
        return_kernel,
        out_shape=jax.ShapeDtypeStruct((2 * TOK + 16, 256), F32),
        in_specs=[vmem] * 5,
        out_specs=vmem,
        compiler_params=pltpu.CompilerParams(vmem_limit_bytes=8 * MIB),
        cost_estimate=cost(100_000_000, 1_500_000),
        name="return_slots",
    )(*parts, routed)


def ring_gather(own):
    left = x_shift(own, 1)
    right = x_shift(own, 3)
    far_a = x_shift(left[: ROWS // 2], 1)
    far_b = x_shift(right[ROWS // 2 :], 3)
    return [own, left, right, far_a, far_b]


def split(value):
    high = lax.reduce_precision(value, 8, 7)
    return high.astype(BF), (value - high).astype(BF)


def on_device(layer_input, out_grad, expert_ids, gate_weights, w_gate, w_up, w_down):
    spot = lax.axis_index("expert")
    chip, core = spot // 2, spot % 2
    x = lax.axis_index("dp") % 4
    where = jnp.stack([x, core]).astype(jnp.int32)
    gate_rows, up_rows, down_rows = w_gate[0], w_up[0], w_down[0]

    relative = (expert_ids - chip) & 3
    picked = relative.T[None] == jnp.arange(EXPERTS, dtype=jnp.int32)[:, None, None]
    named = jnp.sum(picked.astype(F32), axis=1)
    weight = jnp.sum(jnp.where(picked, gate_weights.T.astype(F32)[None], 0.0), axis=1)
    meta = jnp.pad(jnp.concatenate([named, weight]).astype(BF), ((0, 8), (0, 384)))

    def own_columns(half):
        start = x * 512 + half * 256
        a = lax.dynamic_slice(layer_input, (0, start), (TOK, 256))
        b = lax.dynamic_slice(out_grad, (0, start), (TOK, 256))
        return jnp.concatenate([jnp.concatenate([a, b], axis=1), meta], axis=0)

    mine = own_columns(core)
    got = core_swap(own_columns(1 - core))
    filled = fill_slots(where, mine, got)
    zin, zgr, routed, own_grad = filled[:4], filled[4:8], filled[8], filled[9]

    zin = [zin[0]] + [chip_shift(zin[r], r) for r in (1, 2, 3)]
    zgr = [zgr[0]] + [chip_shift(zgr[r], r) for r in (1, 2, 3)]
    in_pieces = ring_gather(jnp.concatenate(zin))
    gr_pieces = ring_gather(jnp.concatenate([z[:PAIR] for z in zgr]))
    gates = jnp.stack([z[PAIR : PAIR + 2, :CAP] for z in zgr]).astype(F32).reshape(ROWS, 1)
    in_pieces = in_pieces + [core_swap(p) for p in in_pieces]
    gr_pieces = gr_pieces + [core_swap(p) for p in gr_pieces]

    rows_input, pre_gate, pre_up = first_work(where, in_pieces, gate_rows, up_rows)
    rows_grad, gpg, upg, scaled, router, keep, send = second_work(
        where, gr_pieces, down_rows, pre_gate, pre_up, gates, gate_rows, up_rows
    )

    summed = keep + core_swap(send).astype(F32)
    router = (router + core_swap(router))[:, 0]
    tail = jnp.stack([jnp.pad(v, (0, 128)) for v in split(router)]).reshape(6, 256)
    tail = jnp.pad(tail, ((0, 10), (0, 0)))
    arrived = [
        x_shift(jnp.concatenate([summed[j].astype(BF), tail]), j).astype(F32) for j in (1, 2, 3)
    ]
    slot_sum = summed[0] + arrived[0][:ROWS] + arrived[1][:ROWS] + arrived[2][:ROWS]
    for a in arrived:
        both = a[ROWS : ROWS + 6].reshape(2, 768)[:, :ROWS]
        router = router + (both[0] + both[1])
    router_hi, router_lo = split(router)
    slot_sum = slot_sum.astype(BF).reshape(EXPERTS, PAIR, 256)
    tails = jnp.stack([v.reshape(EXPERTS, 2, CAP) for v in (router_hi, router_lo)], axis=2)
    tails = jnp.pad(tails.reshape(EXPERTS, 4, CAP), ((0, 0), (0, 12), (0, 256 - CAP)))
    blocks = [jnp.concatenate([slot_sum[r], tails[r]]) for r in range(EXPERTS)]
    blocks = [blocks[0]] + [chip_shift(blocks[r], -r) for r in (1, 2, 3)]

    partial = return_slots(blocks, routed)
    total = partial + pair_swap(partial)
    final = (own_grad.astype(F32) + total[: 2 * TOK].reshape(2, TOK, 256)).astype(BF)
    stays = jnp.where(core == 0, final[0], final[1])
    goes = jnp.where(core == 0, final[1], final[0])
    stays = previous_section(stays, 0)
    goes = previous_section(goes, 1)
    low = jnp.where(core == 0, stays, goes)
    high = jnp.where(core == 0, goes, stays)
    block = jnp.concatenate([low, high], axis=1)
    prev_grad = jnp.zeros((TOK, D), BF)
    for j in range(4):
        piece = block if j == 0 else x_shift(block, j)
        prev_grad = lax.dynamic_update_slice(prev_grad, piece, (0, (x - j) % 4 * 512))

    by_expert = total[2 * TOK :, :TOK]
    by_expert = jnp.where(core == 0, by_expert[:4], by_expert[4:8])
    router_grad = jnp.sum(jnp.where(picked, by_expert[:, None, :], 0.0), axis=0).T

    def weight_grad(a, b):
        return dot(a, b, ((0,), (0,))).astype(BF)[None]

    return (
        prev_grad,
        router_grad,
        weight_grad(gpg, rows_input),
        weight_grad(upg, rows_input),
        weight_grad(scaled, rows_grad),
    )


def solution(mesh):
    tokens = P(("section", "expert"), None)
    units = P("section", ("expert", "dp"), None)
    return jax.shard_map(
        on_device,
        mesh=mesh,
        in_specs=(tokens, tokens, tokens, tokens, units, units, units),
        out_specs=(tokens, tokens, units, units, units),
        check_vma=False,
    )
```

```python
import functools

import jax
import jax.numpy as jnp
from jax import lax
from jax.experimental import pallas as pl
from jax.experimental.pallas import tpu as pltpu
from jax.sharding import PartitionSpec as P

EXPERTS = 4
CAP = 80
TOK = 128
D = 2048
UNITS = 512
ROWS = 640
PAIR = 2 * CAP
AWAY = ROWS - PAIR
HOT = 2 * EXPERTS * CAP
BF = jnp.bfloat16
F32 = jnp.float32
MIB = 1 << 20


def cost(flops, moved):
    return pl.CostEstimate(flops=flops, bytes_accessed=moved, transcendentals=0)


def core_swap(a):
    return lax.ppermute(a, "expert", [(i, i ^ 1) for i in range(8)])


def chip_shift(a, r):
    if r != 2:
        return lax.ppermute(a, "expert", [(i, (i + 2 * r) % 8) for i in range(8)])
    route = [(e * 8 + d, (e + 4) % 8 * 8 + (d + 4) % 8) for e in range(8) for d in range(8)]
    return lax.ppermute(a, ("expert", "dp"), route)


def chip_return(a, r):
    route = []
    for s in range(4):
        for e in range(8):
            for d in range(8):
                to = ((s - 1) % 4 * 8 + (e - 2 * r) % 8) * 8 + (d + (4 if r == 2 else 0)) % 8
                route.append(((s * 8 + e) * 8 + d, to))
    return lax.ppermute(a, ("section", "expert", "dp"), route)


def x_shift(a, j):
    return lax.ppermute(a, "dp", [(i, i // 4 * 4 + (i + j) % 4) for i in range(8)])


def pair_swap(a):
    return lax.ppermute(a, "dp", [(i, (i + 4) % 8) for i in range(8)])


def section_shift(a, by):
    return lax.ppermute(a, "section", [(s, (s + by) % 4) for s in range(4)])


def dot(a, b, dims):
    return lax.dot_general(a, b, (dims, ((), ())), preferred_element_type=F32)


def place_rows(meta):
    earlier = lax.broadcasted_iota(jnp.int32, (TOK, TOK), 0)
    later = lax.broadcasted_iota(jnp.int32, (TOK, TOK), 1)
    upto = (earlier <= later).astype(F32).astype(BF)
    return dot(meta, upto, ((1,), (0,))) - 1.0


def hot_rows(named, place, r):
    slot = lax.broadcasted_iota(jnp.int32, (TOK, TOK), 0).astype(F32)
    hit = (slot == place[r : r + 1]) & (named[r : r + 1] > 0.5)
    return hit.astype(F32).astype(BF)


def slots_kernel(where_ref, mine_ref, got_ref, *outs):
    sends, gate0, pack = outs[:3], outs[3], outs[4]
    core = where_ref[1]
    row = lax.broadcasted_iota(jnp.int32, (16, TOK), 0)
    gate_rows = []
    for c in range(2):
        block = jnp.where(core == c, mine_ref[...].astype(F32), got_ref[...].astype(F32)).astype(BF)
        tokens = block[:TOK]
        meta = block[TOK : TOK + 16, :TOK]
        named = meta.astype(F32)
        place = place_rows(meta)
        for h in range(2):
            at = HOT + (2 * c + h) * TOK
            pack[at : at + TOK, :] = tokens[:, 256 + h * TOK : 384 + h * TOK]
        for r in range(EXPERTS):
            hot = hot_rows(named, place, r)
            at = (c * EXPERTS + r) * CAP
            pack[at : at + CAP, :] = hot[:CAP]
            if r > 0:
                filled = dot(hot[:CAP], tokens, ((1,), (0,))).astype(BF)
                sends[r - 1][c * CAP : (c + 1) * CAP, :] = filled[:, :256]
                sends[r - 1][PAIR + c * CAP : PAIR + (c + 1) * CAP, :] = filled[:, 256:]
            gates = dot(meta, hot, ((1,), (1,)))
            gate_rows.append(gates[4 + r : 5 + r])
    for r in range(EXPERTS):
        tile = jnp.where(row == 0, gate_rows[r], jnp.where(row == 1, gate_rows[4 + r], 0.0))
        if r == 0:
            gate0[...] = tile.astype(BF)
        else:
            sends[r - 1][2 * PAIR :, :TOK] = tile.astype(BF)
            sends[r - 1][2 * PAIR :, TOK:] = jnp.zeros((16, TOK), BF)


BLOCK = pl.BlockSpec()
ANY = pl.BlockSpec(memory_space=pltpu.HBM)
SMEM = pl.BlockSpec(memory_space=pltpu.SMEM)


def params(mib):
    return pltpu.CompilerParams(vmem_limit_bytes=mib * MIB)


def fill_slots(where, mine, got):
    shapes = (
        [jax.ShapeDtypeStruct((2 * PAIR + 16, 256), BF)] * 3
        + [
            jax.ShapeDtypeStruct((16, TOK), BF),
            jax.ShapeDtypeStruct((HOT + 4 * TOK, TOK), BF),
        ]
    )
    return pl.pallas_call(
        slots_kernel,
        out_shape=shapes,
        in_specs=[SMEM] + [BLOCK] * 2,
        out_specs=[BLOCK] * 5,
        compiler_params=params(8),
        cost_estimate=cost(100_000_000, 2_000_000),
        name="fill_slots",
    )(where, mine, got)


def local_kernel(mine_ref, input_ref, grad_ref, out_ref):
    meta = mine_ref[TOK : TOK + 16, :TOK]
    hot = hot_rows(meta.astype(F32), place_rows(meta), 0)[:CAP]
    for at, source in enumerate((input_ref, grad_ref)):
        for part in range(4):
            columns = slice(part * 512, part * 512 + 512)
            out_ref[at, :, columns] = dot(hot, source[:, columns], ((1,), (0,))).astype(BF)


def local_slots(mine, layer_input, out_grad):
    return pl.pallas_call(
        local_kernel,
        out_shape=pltpu.HBM((2, CAP, D), BF),
        in_specs=[BLOCK] * 3,
        out_specs=BLOCK,
        compiler_params=params(8),
        cost_estimate=cost(100_000_000, 2_000_000),
        name="local_slots",
    )(mine, pinned(layer_input), pinned(out_grad))


def column(where_ref, j, flip):
    x, core = where_ref[0], where_ref[1]
    half = core if flip == 0 else 1 - core
    return pl.multiple_of(lax.rem(x + j, 4) * 512 + half * 256, 256)


def copy_all(pairs, sems, first=0):
    copies = [
        pltpu.make_async_copy(source, target, sems.at[first + at])
        for at, (source, target) in enumerate(pairs)
    ]
    for c in copies:
        c.start()
    return copies


def wait_all(copies):
    for c in copies:
        c.wait()


def gather_rows(where_ref, pieces, local, which, whole):
    core = where_ref[1]
    pairs = []
    for flip in range(2):
        half = core if flip == 0 else 1 - core
        rows = pl.ds(pl.multiple_of(half * CAP, 16), CAP)
        pairs.append((local[flip].at[which], whole.at[rows, :]))
        for j, piece in enumerate(pieces[4 * flip : 4 * flip + 4]):
            columns = pl.ds(column(where_ref, (4 - j) % 4, flip), 256)
            pairs.append((piece, whole.at[PAIR:, columns]))
    return pairs


def first_kernel(where_ref, *refs):
    pieces, local, gate_ref, up_ref = refs[:8], refs[8:10], refs[10], refs[11]
    rows_out, pre_gate, pre_up = refs[12:15]
    whole, weights, pre, sems = refs[15:]
    loads = copy_all(
        gather_rows(where_ref, pieces, local, 0, whole)
        + [(gate_ref, weights.at[0]), (up_ref, weights.at[1])],
        sems,
    )
    wait_all(loads[:10])
    stores = copy_all([(whole, rows_out)], sems, 12)
    for at, out in enumerate((pre_gate, pre_up)):
        loads[10 + at].wait()
        for n in range(2):
            units = slice(n * 256, n * 256 + 256)
            pre[at, :, units] = dot(whole[...], weights[at, units, :], ((1,), (1,)))
        stores += copy_all([(pre.at[at], out)], sems, 13 + at)
    wait_all(stores)


def first_work(where, pieces, local, w_gate, w_up):
    return pl.pallas_call(
        first_kernel,
        out_shape=[
            pltpu.HBM((ROWS, D), BF),
            pltpu.HBM((ROWS, UNITS), F32),
            pltpu.HBM((ROWS, UNITS), F32),
        ],
        in_specs=[SMEM] + [ANY] * 12,
        out_specs=[ANY] * 3,
        scratch_shapes=[
            pltpu.VMEM((ROWS, D), BF),
            pltpu.VMEM((2, UNITS, D), BF),
            pltpu.VMEM((2, ROWS, UNITS), F32),
            pltpu.SemaphoreType.DMA((15,)),
        ],
        compiler_params=params(20),
        cost_estimate=cost(2 * 2 * ROWS * D * UNITS, 12_000_000),
        name="first_work",
    )(where, *map(pinned, pieces), *map(pinned, local), w_gate, w_up)


def second_kernel(where_ref, *refs):
    pieces, local = refs[:8], refs[8:10]
    down_ref, pre_gate, pre_up, gates_ref = refs[10:14]
    rows_out, gpg_out, upg_out, scaled_out, router = refs[14:19]
    whole, down, pre, grads, scaled, sems = refs[19:]
    loads = copy_all(
        gather_rows(where_ref, pieces, local, 1, whole)
        + [(down_ref, down), (pre_gate, pre.at[0]), (pre_up, pre.at[1])],
        sems,
    )
    wait_all(loads[:11])
    stores = copy_all([(whole, rows_out)], sems, 13)
    gates = gates_ref[...]
    router_sum = jnp.zeros((ROWS, 1), F32)
    for n in range(2):
        units = slice(n * 256, n * 256 + 256)
        hidden_grad = dot(whole[...], down[units, :], ((1,), (1,)))
        if n == 0:
            wait_all(loads[11:])
        v = pre[0, :, units]
        up = pre[1, :, units]
        s = jax.nn.sigmoid(v)
        activated = v * s
        hidden = activated * up
        router_sum = router_sum + jnp.sum(hidden * hidden_grad, axis=1, keepdims=True)
        scaled_grad = gates * hidden_grad
        grads[0, :, units] = (scaled_grad * up * (s * (1.0 + v * (1.0 - s)))).astype(BF)
        grads[1, :, units] = (scaled_grad * activated).astype(BF)
        scaled[:, units] = (gates * hidden).astype(BF)
    router[...] = router_sum
    stores += copy_all(
        [(grads.at[0], gpg_out), (grads.at[1], upg_out), (scaled, scaled_out)], sems, 14
    )
    wait_all(stores)


def second_work(where, pieces, local, w_down, pre_gate, pre_up, gates):
    return pl.pallas_call(
        second_kernel,
        out_shape=[
            pltpu.HBM((ROWS, D), BF),
            pltpu.HBM((ROWS, UNITS), BF),
            pltpu.HBM((ROWS, UNITS), BF),
            pltpu.HBM((ROWS, UNITS), BF),
            jax.ShapeDtypeStruct((ROWS, 1), F32),
        ],
        in_specs=[SMEM] + [ANY] * 13 + [BLOCK],
        out_specs=[ANY] * 4 + [BLOCK],
        scratch_shapes=[
            pltpu.VMEM((ROWS, D), BF),
            pltpu.VMEM((UNITS, D), BF),
            pltpu.VMEM((2, ROWS, UNITS), F32),
            pltpu.VMEM((2, ROWS, UNITS), BF),
            pltpu.VMEM((ROWS, UNITS), BF),
            pltpu.SemaphoreType.DMA((17,)),
        ],
        compiler_params=params(24),
        cost_estimate=cost(2 * ROWS * D * UNITS, 12_000_000),
        name="second_work",
    )(
        where,
        *map(pinned, pieces),
        *map(pinned, local),
        w_down,
        pinned(pre_gate),
        pinned(pre_up),
        gates,
    )


def give_kernel(where_ref, gate_ref, up_ref, out_ref, held, sems):
    half = 1 - where_ref[1]
    pairs = []
    for at, source in enumerate((gate_ref, up_ref)):
        for part in range(4):
            columns = pl.ds(pl.multiple_of(part * 512 + half * 256, 256), 256)
            target = held.at[at, :, part * 256 : part * 256 + 256]
            pairs.append((source.at[:, columns], target))
    wait_all(copy_all(pairs, sems))
    wait_all(copy_all([(held.at[at], out_ref.at[at]) for at in range(2)], sems, 8))


def give_weights(where, w_gate, w_up):
    return pl.pallas_call(
        give_kernel,
        out_shape=pltpu.HBM((2, UNITS, D // 2), BF),
        in_specs=[SMEM] + [ANY] * 2,
        out_specs=ANY,
        scratch_shapes=[
            pltpu.VMEM((2, UNITS, D // 2), BF),
            pltpu.SemaphoreType.DMA((10,)),
        ],
        compiler_params=params(6),
        cost_estimate=cost(0, 4_000_000),
        name="give_weights",
    )(where, w_gate, w_up)


def part_kernel(chunks, where_ref, *refs):
    sources, gate_ref, up_ref, given, router_a, router_b = refs[:4], *refs[4:9]
    outs, (grads, weights, sems) = refs[9:11], refs[11:]
    x = where_ref[0]
    pairs = [
        (source, grads.at[:, at * UNITS : (at + 1) * UNITS]) for at, source in enumerate(sources)
    ]
    for n, j in enumerate(chunks):
        theirs = pl.ds(pl.multiple_of(lax.rem(x + j, 4) * 256, 256), 256)
        mine = pl.ds(column(where_ref, j, 0), 256)
        blocks = [gate_ref.at[:, mine], up_ref.at[:, mine]]
        blocks += [given.at[0, :, theirs], given.at[1, :, theirs]]
        for at, block in enumerate(blocks):
            rows = slice(at * UNITS, (at + 1) * UNITS)
            pairs.append((block, weights.at[rows, n * 256 : n * 256 + 256]))
    loads = copy_all(pairs, sems)
    wait_all(loads[:4])
    tail = hi_lo(router_a[...] + router_b[...])
    for n, (j, out) in enumerate(zip(chunks, outs)):
        wait_all(loads[4 + 4 * n : 8 + 4 * n])
        total = dot(grads[...], weights[:, n * 256 : n * 256 + 256], ((1,), (0,)))
        if j == 0:
            out[...] = total
        else:
            out[:ROWS, :] = total.astype(BF)
            out[ROWS:, :TOK] = tail
            out[ROWS:, TOK:] = jnp.zeros((16, TOK), BF)


def part_work(chunks, where, grads, w_gate, w_up, given, router_a, router_b):
    shapes = [
        pltpu.HBM((ROWS, 256), F32) if j == 0 else pltpu.HBM((ROWS + 16, 256), BF) for j in chunks
    ]
    return pl.pallas_call(
        functools.partial(part_kernel, chunks),
        out_shape=shapes,
        in_specs=[SMEM] + [ANY] * 7 + [BLOCK] * 2,
        out_specs=[BLOCK] * 2,
        scratch_shapes=[
            pltpu.VMEM((ROWS, 4 * UNITS), BF),
            pltpu.VMEM((4 * UNITS, 512), BF),
            pltpu.SemaphoreType.DMA((12,)),
        ],
        compiler_params=params(16),
        cost_estimate=cost(2 * ROWS * 4 * UNITS * 512, 6_000_000),
        name="part_work",
    )(where, *map(pinned, grads), w_gate, w_up, pinned(given), router_a, router_b)


def hi_lo(value):
    high = value.astype(BF)
    return jnp.concatenate([high.astype(F32), value - high.astype(F32)]).astype(BF)


def x_sum_kernel(where_ref, keep, router_a, router_b, *refs):
    arrived, outs = refs[:3], refs[3:]
    x = where_ref[0]
    own = hi_lo(router_a[...] + router_b[...]).astype(F32)
    tails = [own] + [a[ROWS:, :TOK].astype(F32) for a in arrived]
    tails = [t[:8] + t[8:] for t in tails]
    total = jnp.zeros((8, TOK), F32)
    for at in range(4):
        j = lax.rem(x - at + 4, 4)
        picked = tails[3]
        for k in range(3):
            picked = jnp.where(j == k, tails[k], picked)
        total = total + picked
    tail = hi_lo(total)
    for r in range(EXPERTS):
        rows = slice(r * PAIR, r * PAIR + PAIR)
        block = keep[rows, :]
        for a in arrived:
            block = block + a[rows, :].astype(F32)
        outs[r][:PAIR, :] = block.astype(BF)
        outs[r][PAIR:, :TOK] = tail
        outs[r][PAIR:, TOK:] = jnp.zeros((16, TOK), BF)


def x_sum(where, keep, router_a, router_b, arrived):
    return pl.pallas_call(
        x_sum_kernel,
        out_shape=[jax.ShapeDtypeStruct((PAIR + 16, 256), BF)] * 4,
        in_specs=[SMEM] + [BLOCK] * 6,
        out_specs=[BLOCK] * 4,
        compiler_params=params(8),
        cost_estimate=cost(1_000_000, 3_000_000),
        name="x_sum",
    )(where, pinned(keep), router_a, router_b, *map(pinned, arrived))


def return_kernel(*refs):
    parts, (pack, out_ref) = refs[:4], refs[4:]
    row = lax.broadcasted_iota(jnp.int32, (8, TOK), 0)
    router = jnp.zeros((8, TOK), F32)
    for c in range(2):
        total = jnp.zeros((TOK, 256), F32)
        for r in range(EXPERTS):
            at = (c * EXPERTS + r) * CAP
            hot = pack[at : at + CAP, :]
            total += dot(hot, parts[r][c * CAP : (c + 1) * CAP, :], ((0,), (0,)))
            tail = dot(parts[r][PAIR : PAIR + 16, :CAP], hot, ((1,), (0,)))
            at = 2 * r + c
            value = tail[at : at + 1] + tail[8 + at : 9 + at]
            router = jnp.where(row == 4 * c + r, value, router)
        out_ref[c * TOK : (c + 1) * TOK, :] = total.astype(BF)
    out_ref[2 * TOK :, :TOK] = hi_lo(router)
    out_ref[2 * TOK :, TOK:] = jnp.zeros((16, TOK), BF)


def return_slots(parts, pack):
    return pl.pallas_call(
        return_kernel,
        out_shape=jax.ShapeDtypeStruct((2 * TOK + 16, 256), BF),
        in_specs=[BLOCK] * 5,
        out_specs=BLOCK,
        compiler_params=params(8),
        cost_estimate=cost(100_000_000, 1_500_000),
        name="return_slots",
    )(*parts, pack)


def final_kernel(where_ref, partial, got, pack, stays, goes, router):
    core = where_ref[1]
    total = partial[...].astype(F32) + got[...].astype(F32)
    final = []
    for c in range(2):
        for h in range(2):
            at = HOT + (2 * c + h) * TOK
            columns = slice(h * TOK, h * TOK + TOK)
            rows = total[c * TOK : (c + 1) * TOK, columns]
            final.append(rows + pack[at : at + TOK, :].astype(F32))
    for h in range(2):
        columns = slice(h * TOK, h * TOK + TOK)
        stays[:, columns] = jnp.where(core == 0, final[h], final[2 + h]).astype(BF)
        goes[:, columns] = jnp.where(core == 0, final[2 + h], final[h]).astype(BF)
    tail = total[2 * TOK :, :TOK]
    router[...] = tail[:8] + tail[8:]


def finish(where, partial, got, pack):
    return pl.pallas_call(
        final_kernel,
        out_shape=[
            jax.ShapeDtypeStruct((TOK, 256), BF),
            jax.ShapeDtypeStruct((TOK, 256), BF),
            jax.ShapeDtypeStruct((8, TOK), F32),
        ],
        in_specs=[SMEM] + [BLOCK] * 3,
        out_specs=[BLOCK] * 3,
        compiler_params=params(8),
        cost_estimate=cost(1_000_000, 600_000),
        name="finish",
    )(where, partial, got, pack)


def x_gather(own):
    return [own] + [x_shift(own, j) for j in (1, 2, 3)]


def weight_grad(a, b):
    return dot(a, b, ((0,), (0,))).astype(BF)[None]


def pinned(a):
    return pltpu.with_memory_space_constraint(a, pltpu.HBM)


def on_device(layer_input, out_grad, expert_ids, gate_weights, w_gate, w_up, w_down):
    spot = lax.axis_index("expert")
    chip, core = spot // 2, spot % 2
    x = lax.axis_index("dp") % 4
    where = jnp.stack([x, core]).astype(jnp.int32)
    gate_rows, up_rows, down_rows = pinned(w_gate[0]), pinned(w_up[0]), pinned(w_down[0])

    relative = (expert_ids - chip) & 3
    picked = relative.T[None] == jnp.arange(EXPERTS, dtype=jnp.int32)[:, None, None]
    named = jnp.sum(picked.astype(F32), axis=1)
    weight = jnp.sum(jnp.where(picked, gate_weights.T.astype(F32)[None], 0.0), axis=1)
    meta = jnp.pad(jnp.concatenate([named, weight]).astype(BF), ((0, 8), (0, 384)))

    def own_columns(half):
        start = x * 512 + half * 256
        a = lax.dynamic_slice(layer_input, (0, start), (TOK, 256))
        b = lax.dynamic_slice(out_grad, (0, start), (TOK, 256))
        return jnp.concatenate([jnp.concatenate([a, b], axis=1), meta], axis=0)

    mine = own_columns(core)
    got = core_swap(own_columns(1 - core))
    filled = fill_slots(where, mine, got)
    gate0, pack = filled[3:]
    away = {r: chip_shift(filled[r - 1], r) for r in (2, 1, 3)}
    away = [away[r] for r in (1, 2, 3)]
    given = give_weights(where, gate_rows, up_rows)
    local = local_slots(mine, layer_input, out_grad)
    away, given, local, pack = lax.optimization_barrier(
        (away, given, local, section_shift(pack, -1))
    )
    local = [local, core_swap(local)]
    in_pieces = x_gather(jnp.concatenate([z[:PAIR] for z in away]))
    in_pieces = in_pieces + [core_swap(p) for p in in_pieces]
    gr_pieces = x_gather(jnp.concatenate([z[PAIR : 2 * PAIR] for z in away]))
    gates = jnp.stack([gate0[:2, :CAP]] + [z[2 * PAIR : 2 * PAIR + 2, :CAP] for z in away])
    gates = gates.astype(F32).reshape(ROWS, 1)

    given = core_swap(given)
    rows_input, pre_gate, pre_up = first_work(where, in_pieces, local, gate_rows, up_rows)
    gr_pieces, pre_gate = lax.optimization_barrier((gr_pieces, pre_gate))
    gr_pieces = gr_pieces + [core_swap(p) for p in gr_pieces]
    rows_grad, gpg, upg, scaled, router = second_work(
        where, gr_pieces, local, down_rows, pre_gate, pre_up, gates
    )
    halves = (gpg, upg, core_swap(gpg), core_swap(upg))
    router = jnp.pad(router.reshape(8, CAP), ((0, 0), (0, TOK - CAP)))
    routers = (router, core_swap(router))
    far, near = part_work((2, 1), where, halves, gate_rows, up_rows, given, *routers)
    far, near = x_shift(far, 2), x_shift(near, 1)
    back, keep = part_work((3, 0), where, halves, gate_rows, up_rows, given, *routers)
    gpg, upg, keep = lax.optimization_barrier((gpg, upg, keep))
    arrived = [near, far, x_shift(back, 3)]
    grads = [
        weight_grad(gpg, rows_input),
        weight_grad(upg, rows_input),
        weight_grad(scaled, rows_grad),
    ]
    keep, grads = lax.optimization_barrier((keep, grads))
    blocks = x_sum(where, keep, *routers, arrived)
    blocks = [chip_return(blocks[r], r) for r in range(EXPERTS)]

    partial = return_slots(blocks, pack)
    stays, goes, by_expert = finish(where, partial, pair_swap(partial), pack)
    goes = core_swap(goes)
    low = jnp.where(core == 0, stays, goes)
    high = jnp.where(core == 0, goes, stays)
    block = jnp.concatenate([low, high], axis=1)
    prev_grad = jnp.zeros((TOK, D), BF)
    pieces = [block] + [x_shift(block, j) for j in (1, 2, 3)]
    pieces[1], by_expert = lax.optimization_barrier((pieces[1], by_expert))
    by_expert = section_shift(by_expert, 1)
    for j, piece in enumerate(pieces):
        prev_grad = lax.dynamic_update_slice(prev_grad, piece, (0, (x - j) % 4 * 512))
    by_expert = jnp.where(core == 0, by_expert[:4], by_expert[4:])
    router_grad = jnp.sum(jnp.where(picked, by_expert[:, None, :], 0.0), axis=0).T
    return (prev_grad, router_grad, *grads)


def solution(mesh):
    tokens = P(("section", "expert"), None)
    units = P("section", ("expert", "dp"), None)
    return jax.shard_map(
        on_device,
        mesh=mesh,
        in_specs=(tokens, tokens, tokens, tokens, units, units, units),
        out_specs=(tokens, tokens, units, units, units),
        check_vma=False,
    )
```

```python
import functools

import jax
import jax.numpy as jnp
from jax import lax
from jax.experimental import pallas as pl
from jax.experimental.pallas import tpu as pltpu
from jax.sharding import PartitionSpec as P

EXPERTS = 4
CAP = 80
TOK = 128
D = 2048
UNITS = 512
ROWS = 640
PAIR = 2 * CAP
AWAY = ROWS - PAIR
HOT = 2 * EXPERTS * CAP
BF = jnp.bfloat16
F32 = jnp.float32
MIB = 1 << 20


def cost(flops, moved):
    return pl.CostEstimate(flops=flops, bytes_accessed=moved, transcendentals=0)


def core_swap(a):
    return lax.ppermute(a, "expert", [(i, i ^ 1) for i in range(8)])


def chip_shift(a, r):
    if r != 2:
        return lax.ppermute(a, "expert", [(i, (i + 2 * r) % 8) for i in range(8)])
    route = [(e * 8 + d, (e + 4) % 8 * 8 + (d + 4) % 8) for e in range(8) for d in range(8)]
    return lax.ppermute(a, ("expert", "dp"), route)


def chip_return(a, r):
    route = []
    for s in range(4):
        for e in range(8):
            for d in range(8):
                to = ((s - 1) % 4 * 8 + (e - 2 * r) % 8) * 8 + (d + (4 if r == 2 else 0)) % 8
                route.append(((s * 8 + e) * 8 + d, to))
    return lax.ppermute(a, ("section", "expert", "dp"), route)


def x_shift(a, j):
    return lax.ppermute(a, "dp", [(i, i // 4 * 4 + (i + j) % 4) for i in range(8)])


def pair_swap(a):
    return lax.ppermute(a, "dp", [(i, (i + 4) % 8) for i in range(8)])


def section_shift(a, by):
    return lax.ppermute(a, "section", [(s, (s + by) % 4) for s in range(4)])


def next_section_pair(a):
    route = [(s * 8 + d, (s + 1) % 4 * 8 + (d + 4) % 8) for s in range(4) for d in range(8)]
    return lax.ppermute(a, ("section", "dp"), route)


def dot(a, b, dims):
    return lax.dot_general(a, b, (dims, ((), ())), preferred_element_type=F32)


def place_rows(meta):
    earlier = lax.broadcasted_iota(jnp.int32, (TOK, TOK), 0)
    later = lax.broadcasted_iota(jnp.int32, (TOK, TOK), 1)
    upto = (earlier <= later).astype(F32).astype(BF)
    return dot(meta, upto, ((1,), (0,))) - 1.0


def hot_rows(named, place, r):
    slot = lax.broadcasted_iota(jnp.int32, (TOK, TOK), 0).astype(F32)
    hit = (slot == place[r : r + 1]) & (named[r : r + 1] > 0.5)
    return hit.astype(F32).astype(BF)


def slots_kernel(where_ref, mine_ref, got_ref, *outs):
    sends, gate0, pack = outs[:3], outs[3], outs[4]
    core = where_ref[1]
    row = lax.broadcasted_iota(jnp.int32, (16, TOK), 0)
    gate_rows = []
    for c in range(2):
        block = jnp.where(core == c, mine_ref[...].astype(F32), got_ref[...].astype(F32)).astype(BF)
        tokens = block[:TOK]
        meta = block[TOK : TOK + 16, :TOK]
        named = meta.astype(F32)
        place = place_rows(meta)
        for h in range(2):
            at = HOT + (2 * c + h) * TOK
            pack[at : at + TOK, :] = tokens[:, 256 + h * TOK : 384 + h * TOK]
        for r in range(EXPERTS):
            hot = hot_rows(named, place, r)
            at = (c * EXPERTS + r) * CAP
            pack[at : at + CAP, :] = hot[:CAP]
            if r > 0:
                filled = dot(hot[:CAP], tokens, ((1,), (0,))).astype(BF)
                sends[r - 1][c * CAP : (c + 1) * CAP, :] = filled[:, :256]
                sends[r - 1][PAIR + c * CAP : PAIR + (c + 1) * CAP, :] = filled[:, 256:]
            gates = dot(meta, hot, ((1,), (1,)))
            gate_rows.append(gates[4 + r : 5 + r])
    for r in range(EXPERTS):
        tile = jnp.where(row == 0, gate_rows[r], jnp.where(row == 1, gate_rows[4 + r], 0.0))
        if r == 0:
            gate0[...] = tile.astype(BF)
        else:
            sends[r - 1][2 * PAIR :, :TOK] = tile.astype(BF)
            sends[r - 1][2 * PAIR :, TOK:] = jnp.zeros((16, TOK), BF)


BLOCK = pl.BlockSpec()
VMEM = pl.BlockSpec(memory_space=pltpu.VMEM)
ANY = pl.BlockSpec(memory_space=pltpu.HBM)
SMEM = pl.BlockSpec(memory_space=pltpu.SMEM)


def params(mib):
    return pltpu.CompilerParams(vmem_limit_bytes=mib * MIB)


def fill_slots(where, mine, got):
    shapes = (
        [jax.ShapeDtypeStruct((2 * PAIR + 16, 256), BF)] * 3
        + [
            jax.ShapeDtypeStruct((16, TOK), BF),
            jax.ShapeDtypeStruct((HOT + 4 * TOK, TOK), BF),
        ]
    )
    return pl.pallas_call(
        slots_kernel,
        out_shape=shapes,
        in_specs=[SMEM] + [BLOCK] * 2,
        out_specs=[BLOCK] * 5,
        compiler_params=params(8),
        cost_estimate=cost(100_000_000, 2_000_000),
        name="fill_slots",
    )(where, mine, got)


def local_kernel(mine_ref, input_ref, grad_ref, out_ref):
    meta = mine_ref[TOK : TOK + 16, :TOK]
    hot = hot_rows(meta.astype(F32), place_rows(meta), 0)[:CAP]
    for at, source in enumerate((input_ref, grad_ref)):
        for part in range(4):
            columns = slice(part * 512, part * 512 + 512)
            out_ref[at, :, columns] = dot(hot, source[:, columns], ((1,), (0,))).astype(BF)


def local_slots(mine, layer_input, out_grad):
    return pl.pallas_call(
        local_kernel,
        out_shape=pltpu.HBM((2, CAP, D), BF),
        in_specs=[BLOCK] * 3,
        out_specs=BLOCK,
        compiler_params=params(8),
        cost_estimate=cost(100_000_000, 2_000_000),
        name="local_slots",
    )(mine, pinned(layer_input), pinned(out_grad))


def column(where_ref, j, flip):
    x, core = where_ref[0], where_ref[1]
    half = core if flip == 0 else 1 - core
    return pl.multiple_of(lax.rem(x + j, 4) * 512 + half * 256, 256)


def copy_all(pairs, sems, first=0):
    copies = [
        pltpu.make_async_copy(source, target, sems.at[first + at])
        for at, (source, target) in enumerate(pairs)
    ]
    for c in copies:
        c.start()
    return copies


def wait_all(copies):
    for c in copies:
        c.wait()


def gather_rows(where_ref, pieces, local, which, whole):
    core = where_ref[1]
    pairs = []
    for flip in range(2):
        half = core if flip == 0 else 1 - core
        rows = pl.ds(pl.multiple_of(half * CAP, 16), CAP)
        pairs.append((local[flip].at[which], whole.at[rows, :]))
        for j, piece in enumerate(pieces[4 * flip : 4 * flip + 4]):
            columns = pl.ds(column(where_ref, (4 - j) % 4, flip), 256)
            rows = slice(which * AWAY, which * AWAY + AWAY)
            pairs.append((piece.at[rows, :], whole.at[PAIR:, columns]))
    return pairs


def expert_kernel(where_ref, *refs):
    pieces, local = refs[:8], refs[8:10]
    gate_rows, up_rows, down_rows, gates_ref = refs[10:14]
    input_out, grad_out, gpg_out, upg_out, scaled_out, router, grads = refs[14:21]
    inputs, out_grads, scaled, sems = refs[21:]
    loads = copy_all(
        gather_rows(where_ref, pieces, local, 0, inputs)
        + gather_rows(where_ref, pieces, local, 1, out_grads),
        sems,
    )
    wait_all(loads[:10])
    stores = copy_all([(inputs, input_out)], sems, 20)
    gates = gates_ref[...]
    router_sum = jnp.zeros((ROWS, 1), F32)
    for n in range(2):
        units = slice(n * 256, n * 256 + 256)
        ups = slice(UNITS + n * 256, UNITS + n * 256 + 256)
        v = dot(inputs[...], gate_rows[units, :], ((1,), (1,)))
        up = dot(inputs[...], up_rows[units, :], ((1,), (1,)))
        if n == 0:
            wait_all(loads[10:])
            stores += copy_all([(out_grads, grad_out)], sems, 21)
        hidden_grad = dot(out_grads[...], down_rows[units, :], ((1,), (1,)))
        s = jax.nn.sigmoid(v)
        activated = v * s
        hidden = activated * up
        router_sum = router_sum + jnp.sum(hidden * hidden_grad, axis=1, keepdims=True)
        scaled_grad = gates * hidden_grad
        grads[:, units] = (scaled_grad * up * (s * (1.0 + v * (1.0 - s)))).astype(BF)
        grads[:, ups] = (scaled_grad * activated).astype(BF)
        scaled[:, units] = (gates * hidden).astype(BF)
        stores += copy_all(
            [
                (grads.at[:, units], gpg_out.at[:, units]),
                (grads.at[:, ups], upg_out.at[:, units]),
                (scaled.at[:, units], scaled_out.at[:, units]),
            ],
            sems,
            22 + 3 * n,
        )
    router[...] = router_sum
    wait_all(stores)


def expert_work(where, pieces, local, w_gate, w_up, w_down, gates):
    return pl.pallas_call(
        expert_kernel,
        out_shape=[
            pltpu.HBM((ROWS, D), BF),
            pltpu.HBM((ROWS, D), BF),
            pltpu.HBM((ROWS, UNITS), BF),
            pltpu.HBM((ROWS, UNITS), BF),
            pltpu.HBM((ROWS, UNITS), BF),
            jax.ShapeDtypeStruct((ROWS, 1), F32),
            jax.ShapeDtypeStruct((ROWS, 2 * UNITS), BF),
        ],
        in_specs=[SMEM] + [ANY] * 10 + [VMEM] * 4,
        out_specs=[ANY] * 5 + [VMEM] * 2,
        scratch_shapes=[
            pltpu.VMEM((ROWS, D), BF),
            pltpu.VMEM((ROWS, D), BF),
            pltpu.VMEM((ROWS, UNITS), BF),
            pltpu.SemaphoreType.DMA((28,)),
        ],
        compiler_params=params(16),
        cost_estimate=cost(3 * 2 * ROWS * D * UNITS, 12_000_000),
        name="expert_work",
    )(where, *map(pinned, pieces), *map(pinned, local), w_gate, w_up, w_down, gates)


CHUNKS = ((2, 1), (3, 0))


def arrange_kernel(where_ref, gate_ref, up_ref, *refs):
    outs, (held, sems) = refs[:4], refs[4:]
    pairs = []
    for n in range(4):
        chunks = CHUNKS[n % 2]
        for h, j in enumerate(chunks):
            columns = pl.ds(column(where_ref, j, n // 2), 256)
            for at, source in enumerate((gate_ref, up_ref)):
                rows = slice(at * UNITS, (at + 1) * UNITS)
                target = held.at[n, h, rows, :]
                pairs.append((source.at[:, columns], target))
    loads = copy_all(pairs, sems)
    stores = []
    for n in range(4):
        wait_all(loads[4 * n : 4 * n + 4])
        stores += copy_all([(held.at[n], outs[n])], sems, 16 + n)
    wait_all(stores)


def arrange_weights(where, w_gate, w_up):
    return pl.pallas_call(
        arrange_kernel,
        out_shape=[pltpu.HBM((2, 2 * UNITS, 256), BF)] * 4,
        in_specs=[SMEM] + [ANY] * 2,
        out_specs=[ANY] * 4,
        scratch_shapes=[
            pltpu.VMEM((4, 2, 2 * UNITS, 256), BF),
            pltpu.SemaphoreType.DMA((20,)),
        ],
        compiler_params=params(8),
        cost_estimate=cost(0, 8_000_000),
        name="arrange_weights",
    )(where, w_gate, w_up)


def part_kernel(chunks, grads, got, own, given, router_a, router_b, *outs):
    tail = hi_lo(router_a[...] + router_b[...])
    for n, (j, out) in enumerate(zip(chunks, outs)):
        total = dot(grads[...], own[n], ((1,), (0,)))
        total = total + dot(got[...], given[n], ((1,), (0,)))
        if j == 0:
            out[...] = total
        else:
            out[:ROWS, :] = total.astype(BF)
            out[ROWS:, :TOK] = tail
            out[ROWS:, TOK:] = jnp.zeros((16, TOK), BF)


def part_work(chunks, grads, got, own, given, router_a, router_b):
    shapes = [
        jax.ShapeDtypeStruct((ROWS, 256), F32)
        if j == 0
        else jax.ShapeDtypeStruct((ROWS + 16, 256), BF)
        for j in chunks
    ]
    return pl.pallas_call(
        functools.partial(part_kernel, chunks),
        out_shape=shapes,
        in_specs=[VMEM] * 6,
        out_specs=[VMEM] * 2,
        compiler_params=params(8),
        cost_estimate=cost(2 * ROWS * 4 * UNITS * 512, 6_000_000),
        name="part_work",
    )(grads, got, own, given, router_a, router_b)


def hi_lo(value):
    high = value.astype(BF)
    return jnp.concatenate([high.astype(F32), value - high.astype(F32)]).astype(BF)


def x_sum_kernel(where_ref, keep, router_a, router_b, *refs):
    arrived, outs = refs[:3], refs[3:]
    x = where_ref[0]
    own = hi_lo(router_a[...] + router_b[...]).astype(F32)
    tails = [own] + [a[ROWS:, :TOK].astype(F32) for a in arrived]
    tails = [t[:8] + t[8:] for t in tails]
    total = jnp.zeros((8, TOK), F32)
    for at in range(4):
        j = lax.rem(x - at + 4, 4)
        picked = tails[3]
        for k in range(3):
            picked = jnp.where(j == k, tails[k], picked)
        total = total + picked
    tail = hi_lo(total)
    for r in range(EXPERTS):
        rows = slice(r * PAIR, r * PAIR + PAIR)
        block = keep[rows, :]
        for a in arrived:
            block = block + a[rows, :].astype(F32)
        outs[r][:PAIR, :] = block.astype(BF)
        outs[r][PAIR:, :TOK] = tail
        outs[r][PAIR:, TOK:] = jnp.zeros((16, TOK), BF)


def x_sum(where, keep, router_a, router_b, arrived):
    return pl.pallas_call(
        x_sum_kernel,
        out_shape=[jax.ShapeDtypeStruct((PAIR + 16, 256), BF)] * 4,
        in_specs=[SMEM] + [VMEM] * 6,
        out_specs=[BLOCK] * 4,
        compiler_params=params(8),
        cost_estimate=cost(1_000_000, 3_000_000),
        name="x_sum",
    )(where, keep, router_a, router_b, *arrived)


def return_kernel(*refs):
    parts, (pack, out_ref, router_ref) = refs[:4], refs[4:]
    row = lax.broadcasted_iota(jnp.int32, (8, TOK), 0)
    router = jnp.zeros((8, TOK), F32)
    for c in range(2):
        total = jnp.zeros((TOK, 256), F32)
        for r in range(EXPERTS):
            at = (c * EXPERTS + r) * CAP
            hot = pack[at : at + CAP, :]
            total += dot(hot, parts[r][c * CAP : (c + 1) * CAP, :], ((0,), (0,)))
            tail = dot(parts[r][PAIR : PAIR + 16, :CAP], hot, ((1,), (0,)))
            at = 2 * r + c
            value = tail[at : at + 1] + tail[8 + at : 9 + at]
            router = jnp.where(row == 4 * c + r, value, router)
        out_ref[c * TOK : (c + 1) * TOK, :] = total.astype(BF)
    router_ref[...] = router


def return_slots(parts, pack):
    return pl.pallas_call(
        return_kernel,
        out_shape=[
            jax.ShapeDtypeStruct((2 * TOK, 256), BF),
            jax.ShapeDtypeStruct((8, TOK), F32),
        ],
        in_specs=[BLOCK] * 5,
        out_specs=[BLOCK] * 2,
        compiler_params=params(8),
        cost_estimate=cost(100_000_000, 1_500_000),
        name="return_slots",
    )(*parts, pack)


def final_kernel(where_ref, partial, got, pack, stays, goes):
    core = where_ref[1]
    total = partial[...].astype(F32) + got[...].astype(F32)
    final = []
    for c in range(2):
        for h in range(2):
            at = HOT + (2 * c + h) * TOK
            columns = slice(h * TOK, h * TOK + TOK)
            rows = total[c * TOK : (c + 1) * TOK, columns]
            final.append(rows + pack[at : at + TOK, :].astype(F32))
    for h in range(2):
        columns = slice(h * TOK, h * TOK + TOK)
        stays[:, columns] = jnp.where(core == 0, final[h], final[2 + h]).astype(BF)
        goes[:, columns] = jnp.where(core == 0, final[2 + h], final[h]).astype(BF)


def finish(where, partial, got, pack):
    return pl.pallas_call(
        final_kernel,
        out_shape=[
            jax.ShapeDtypeStruct((TOK, 256), BF),
            jax.ShapeDtypeStruct((TOK, 256), BF),
        ],
        in_specs=[SMEM] + [BLOCK] * 3,
        out_specs=[BLOCK] * 2,
        compiler_params=params(8),
        cost_estimate=cost(1_000_000, 600_000),
        name="finish",
    )(where, partial, got, pack)


def x_gather(own):
    return [own] + [x_shift(own, j) for j in (1, 2, 3)]


def weight_grad(a, b):
    return dot(a, b, ((0,), (0,))).astype(BF)[None]


def pinned(a):
    return pltpu.with_memory_space_constraint(a, pltpu.HBM)


def on_device(layer_input, out_grad, expert_ids, gate_weights, w_gate, w_up, w_down):
    spot = lax.axis_index("expert")
    chip, core = spot // 2, spot % 2
    x = lax.axis_index("dp") % 4
    where = jnp.stack([x, core]).astype(jnp.int32)
    gate_rows, up_rows = pinned(w_gate[0]), pinned(w_up[0])

    relative = (expert_ids - chip) & 3
    picked = relative.T[None] == jnp.arange(EXPERTS, dtype=jnp.int32)[:, None, None]
    named = jnp.sum(picked.astype(F32), axis=1)
    weight = jnp.sum(jnp.where(picked, gate_weights.T.astype(F32)[None], 0.0), axis=1)
    meta = jnp.pad(jnp.concatenate([named, weight]).astype(BF), ((0, 8), (0, 384)))

    def own_columns(half):
        start = x * 512 + half * 256
        a = lax.dynamic_slice(layer_input, (0, start), (TOK, 256))
        b = lax.dynamic_slice(out_grad, (0, start), (TOK, 256))
        return jnp.concatenate([jnp.concatenate([a, b], axis=1), meta], axis=0)

    mine = own_columns(core)
    got = core_swap(own_columns(1 - core))
    filled = fill_slots(where, mine, got)
    gate0, pack = filled[3:]
    away = {r: chip_shift(filled[r - 1], r) for r in (2, 1, 3)}
    away = [away[r] for r in (1, 2, 3)]
    own_a, own_b, give_a, give_b = arrange_weights(where, gate_rows, up_rows)
    local = local_slots(mine, layer_input, out_grad)
    away, given, local = lax.optimization_barrier((away, [give_a, give_b], local))
    local = [local, core_swap(local)]
    rows = [z[:PAIR] for z in away] + [z[PAIR : 2 * PAIR] for z in away]
    pieces = x_gather(jnp.concatenate(rows))
    own, near, given, pack = lax.optimization_barrier((pieces[0], pieces[1], given, pack))
    pack = section_shift(pack, -1)
    given = [pinned(core_swap(g)) for g in given]
    pieces[:2] = own, near
    gates = jnp.stack([gate0[:2, :CAP]] + [z[2 * PAIR : 2 * PAIR + 2, :CAP] for z in away])
    gates = gates.astype(F32).reshape(ROWS, 1)
    pieces = pieces + [core_swap(p) for p in pieces]
    pieces, given, pack = lax.optimization_barrier((pieces, given, pack))

    rows_input, rows_grad, gpg, upg, scaled, router, half = expert_work(
        where, pieces, local, w_gate[0], w_up[0], w_down[0], gates
    )
    got = core_swap(half)
    router = jnp.pad(router.reshape(8, CAP), ((0, 0), (0, TOK - CAP)))
    routers = (router, core_swap(router))
    far, near = part_work(CHUNKS[0], half, got, own_a, given[0], *routers)
    far, near = x_shift(far, 2), x_shift(near, 1)
    back, keep = part_work(CHUNKS[1], half, got, own_b, given[1], *routers)
    gpg, upg, scaled, keep = lax.optimization_barrier((gpg, upg, scaled, keep))
    arrived = [near, far, x_shift(back, 3)]
    grads = [weight_grad(gpg, rows_input), weight_grad(upg, rows_input)]
    keep, grads = lax.optimization_barrier((keep, grads))
    blocks = x_sum(where, keep, *routers, arrived)
    blocks, scaled = lax.optimization_barrier((blocks, scaled))
    blocks = [chip_return(blocks[r], r) for r in range(EXPERTS)]
    grads.append(weight_grad(scaled, rows_grad))
    blocks, grads = lax.optimization_barrier((blocks, grads))

    partial, by_expert = return_slots(blocks, pack)
    by_expert = section_shift(by_expert, 1) + next_section_pair(by_expert)
    stays, goes = finish(where, partial, pair_swap(partial), pack)
    goes, by_expert = lax.optimization_barrier((goes, by_expert))
    goes = core_swap(goes)
    low = jnp.where(core == 0, stays, goes)
    high = jnp.where(core == 0, goes, stays)
    block = jnp.concatenate([low, high], axis=1)
    prev_grad = jnp.zeros((TOK, D), BF)
    pieces = [block] + [x_shift(block, j) for j in (1, 2, 3)]
    for j, piece in enumerate(pieces):
        prev_grad = lax.dynamic_update_slice(prev_grad, piece, (0, (x - j) % 4 * 512))
    by_expert = jnp.where(core == 0, by_expert[:4], by_expert[4:])
    router_grad = jnp.sum(jnp.where(picked, by_expert[:, None, :], 0.0), axis=0).T
    return (prev_grad, router_grad, *grads)


def solution(mesh):
    tokens = P(("section", "expert"), None)
    units = P("section", ("expert", "dp"), None)
    return jax.shard_map(
        on_device,
        mesh=mesh,
        in_specs=(tokens, tokens, tokens, tokens, units, units, units),
        out_specs=(tokens, tokens, units, units, units),
        check_vma=False,
    )
```

```python
import functools

import jax
import jax.numpy as jnp
from jax import lax
from jax.experimental import pallas as pl
from jax.experimental.pallas import tpu as pltpu
from jax.sharding import PartitionSpec as P

EXPERTS = 4
CAP = 80
TOK = 128
D = 2048
UNITS = 512
ROWS = 640
PAIR = 2 * CAP
AWAY = ROWS - PAIR
HOT = 2 * EXPERTS * CAP
BF = jnp.bfloat16
F32 = jnp.float32
MIB = 1 << 20


def cost(flops, moved):
    return pl.CostEstimate(flops=flops, bytes_accessed=moved, transcendentals=0)


def core_swap(a):
    return lax.ppermute(a, "expert", [(i, i ^ 1) for i in range(8)])


def chip_shift(a, r):
    if r != 2:
        return lax.ppermute(a, "expert", [(i, (i + 2 * r) % 8) for i in range(8)])
    route = [(e * 8 + d, (e + 4) % 8 * 8 + (d + 4) % 8) for e in range(8) for d in range(8)]
    return lax.ppermute(a, ("expert", "dp"), route)


def chip_return(a, r):
    route = []
    for s in range(4):
        for e in range(8):
            for d in range(8):
                to = ((s - 1) % 4 * 8 + (e - 2 * r) % 8) * 8 + (d + (4 if r == 2 else 0)) % 8
                route.append(((s * 8 + e) * 8 + d, to))
    return lax.ppermute(a, ("section", "expert", "dp"), route)


def x_shift(a, j):
    return lax.ppermute(a, "dp", [(i, i // 4 * 4 + (i + j) % 4) for i in range(8)])


def pair_swap(a):
    return lax.ppermute(a, "dp", [(i, (i + 4) % 8) for i in range(8)])


def section_shift(a, by):
    return lax.ppermute(a, "section", [(s, (s + by) % 4) for s in range(4)])


def dot(a, b, dims):
    return lax.dot_general(a, b, (dims, ((), ())), preferred_element_type=F32)


def place_rows(meta):
    earlier = lax.broadcasted_iota(jnp.int32, (TOK, TOK), 0)
    later = lax.broadcasted_iota(jnp.int32, (TOK, TOK), 1)
    upto = (earlier <= later).astype(F32).astype(BF)
    return dot(meta, upto, ((1,), (0,))) - 1.0


def hot_rows(named, place, r):
    slot = lax.broadcasted_iota(jnp.int32, (TOK, TOK), 0).astype(F32)
    hit = (slot == place[r : r + 1]) & (named[r : r + 1] > 0.5)
    return hit.astype(F32).astype(BF)


def slots_kernel(where_ref, mine_ref, got_ref, *outs):
    sends, gate0, pack = outs[:3], outs[3], outs[4]
    core = where_ref[1]
    row = lax.broadcasted_iota(jnp.int32, (16, TOK), 0)
    gate_rows = []
    for c in range(2):
        block = jnp.where(core == c, mine_ref[...].astype(F32), got_ref[...].astype(F32)).astype(BF)
        tokens = block[:TOK]
        meta = block[TOK : TOK + 16, :TOK]
        named = meta.astype(F32)
        place = place_rows(meta)
        for h in range(2):
            at = HOT + (2 * c + h) * TOK
            pack[at : at + TOK, :] = tokens[:, 256 + h * TOK : 384 + h * TOK]
        for r in range(EXPERTS):
            hot = hot_rows(named, place, r)
            at = (c * EXPERTS + r) * CAP
            pack[at : at + CAP, :] = hot[:CAP]
            if r > 0:
                filled = dot(hot[:CAP], tokens, ((1,), (0,))).astype(BF)
                sends[r - 1][c * CAP : (c + 1) * CAP, :] = filled[:, :256]
                sends[r - 1][PAIR + c * CAP : PAIR + (c + 1) * CAP, :] = filled[:, 256:]
            gates = dot(meta, hot, ((1,), (1,)))
            gate_rows.append(gates[4 + r : 5 + r])
    for r in range(EXPERTS):
        tile = jnp.where(row == 0, gate_rows[r], jnp.where(row == 1, gate_rows[4 + r], 0.0))
        if r == 0:
            gate0[...] = tile.astype(BF)
        else:
            sends[r - 1][2 * PAIR :, :TOK] = tile.astype(BF)
            sends[r - 1][2 * PAIR :, TOK:] = jnp.zeros((16, TOK), BF)


BLOCK = pl.BlockSpec()
VMEM = pl.BlockSpec(memory_space=pltpu.VMEM)
ANY = pl.BlockSpec(memory_space=pltpu.HBM)
SMEM = pl.BlockSpec(memory_space=pltpu.SMEM)


def params(mib):
    return pltpu.CompilerParams(vmem_limit_bytes=mib * MIB)


def fill_slots(where, mine, got):
    shapes = (
        [jax.ShapeDtypeStruct((2 * PAIR + 16, 256), BF)] * 3
        + [
            jax.ShapeDtypeStruct((16, TOK), BF),
            jax.ShapeDtypeStruct((HOT + 4 * TOK, TOK), BF),
        ]
    )
    return pl.pallas_call(
        slots_kernel,
        out_shape=shapes,
        in_specs=[SMEM] + [BLOCK] * 2,
        out_specs=[BLOCK] * 5,
        compiler_params=params(8),
        cost_estimate=cost(100_000_000, 2_000_000),
        name="fill_slots",
    )(where, mine, got)


def local_kernel(mine_ref, input_ref, grad_ref, out_ref):
    meta = mine_ref[TOK : TOK + 16, :TOK]
    hot = hot_rows(meta.astype(F32), place_rows(meta), 0)[:CAP]
    for at, source in enumerate((input_ref, grad_ref)):
        for part in range(4):
            columns = slice(part * 512, part * 512 + 512)
            out_ref[at, :, columns] = dot(hot, source[:, columns], ((1,), (0,))).astype(BF)


def local_slots(mine, layer_input, out_grad):
    return pl.pallas_call(
        local_kernel,
        out_shape=pltpu.HBM((2, CAP, D), BF),
        in_specs=[BLOCK] * 3,
        out_specs=BLOCK,
        compiler_params=params(8),
        cost_estimate=cost(100_000_000, 2_000_000),
        name="local_slots",
    )(mine, pinned(layer_input), pinned(out_grad))


def column(where_ref, j, flip):
    x, core = where_ref[0], where_ref[1]
    half = core if flip == 0 else 1 - core
    return pl.multiple_of(lax.rem(x + j, 4) * 512 + half * 256, 256)


def copy_all(pairs, sems, first=0):
    copies = [
        pltpu.make_async_copy(source, target, sems.at[first + at])
        for at, (source, target) in enumerate(pairs)
    ]
    for c in copies:
        c.start()
    return copies


def wait_all(copies):
    for c in copies:
        c.wait()


def gather_rows(where_ref, pieces, local, which, whole):
    core = where_ref[1]
    pairs = []
    for flip in range(2):
        half = core if flip == 0 else 1 - core
        rows = pl.ds(pl.multiple_of(half * CAP, 16), CAP)
        pairs.append((local[flip].at[which], whole.at[rows, :]))
        for j, piece in enumerate(pieces[4 * flip : 4 * flip + 4]):
            columns = pl.ds(column(where_ref, (4 - j) % 4, flip), 256)
            rows = slice(which * AWAY, which * AWAY + AWAY)
            pairs.append((piece.at[rows, :], whole.at[PAIR:, columns]))
    return pairs


def expert_kernel(where_ref, *refs):
    pieces, local = refs[:8], refs[8:10]
    gate_rows, up_rows, down_rows, gates_ref = refs[10:14]
    input_out, grad_out, gpg_out, upg_out, scaled_out, router, grads = refs[14:21]
    inputs, out_grads, scaled, sems = refs[21:]
    loads = copy_all(
        gather_rows(where_ref, pieces, local, 0, inputs)
        + gather_rows(where_ref, pieces, local, 1, out_grads),
        sems,
    )
    wait_all(loads[:10])
    stores = copy_all([(inputs, input_out)], sems, 20)
    gates = gates_ref[...]
    router_sum = jnp.zeros((ROWS, 1), F32)
    for n in range(2):
        units = slice(n * 256, n * 256 + 256)
        ups = slice(UNITS + n * 256, UNITS + n * 256 + 256)
        v = dot(inputs[...], gate_rows[units, :], ((1,), (1,)))
        up = dot(inputs[...], up_rows[units, :], ((1,), (1,)))
        if n == 0:
            wait_all(loads[10:])
            stores += copy_all([(out_grads, grad_out)], sems, 21)
        hidden_grad = dot(out_grads[...], down_rows[units, :], ((1,), (1,)))
        s = jax.nn.sigmoid(v)
        activated = v * s
        hidden = activated * up
        router_sum = router_sum + jnp.sum(hidden * hidden_grad, axis=1, keepdims=True)
        scaled_grad = gates * hidden_grad
        grads[:, units] = (scaled_grad * up * (s * (1.0 + v * (1.0 - s)))).astype(BF)
        grads[:, ups] = (scaled_grad * activated).astype(BF)
        scaled[:, units] = (gates * hidden).astype(BF)
        stores += copy_all(
            [
                (grads.at[:, units], gpg_out.at[:, units]),
                (grads.at[:, ups], upg_out.at[:, units]),
                (scaled.at[:, units], scaled_out.at[:, units]),
            ],
            sems,
            22 + 3 * n,
        )
    router[...] = router_sum
    wait_all(stores)


def expert_work(where, pieces, local, w_gate, w_up, w_down, gates):
    return pl.pallas_call(
        expert_kernel,
        out_shape=[
            pltpu.HBM((ROWS, D), BF),
            pltpu.HBM((ROWS, D), BF),
            pltpu.HBM((ROWS, UNITS), BF),
            pltpu.HBM((ROWS, UNITS), BF),
            pltpu.HBM((ROWS, UNITS), BF),
            jax.ShapeDtypeStruct((ROWS, 1), F32),
            jax.ShapeDtypeStruct((ROWS, 2 * UNITS), BF),
        ],
        in_specs=[SMEM] + [ANY] * 10 + [VMEM] * 4,
        out_specs=[ANY] * 5 + [VMEM] * 2,
        scratch_shapes=[
            pltpu.VMEM((ROWS, D), BF),
            pltpu.VMEM((ROWS, D), BF),
            pltpu.VMEM((ROWS, UNITS), BF),
            pltpu.SemaphoreType.DMA((28,)),
        ],
        compiler_params=params(16),
        cost_estimate=cost(3 * 2 * ROWS * D * UNITS, 12_000_000),
        name="expert_work",
    )(where, *map(pinned, pieces), *map(pinned, local), w_gate, w_up, w_down, gates)


CHUNKS = ((2, 1), (3, 0))


def arrange_kernel(where_ref, gate_ref, up_ref, *refs):
    outs, (held, sems) = refs[:4], refs[4:]
    pairs = []
    for n in range(4):
        chunks = CHUNKS[n % 2]
        for h, j in enumerate(chunks):
            columns = pl.ds(column(where_ref, j, n // 2), 256)
            for at, source in enumerate((gate_ref, up_ref)):
                rows = slice(at * UNITS, (at + 1) * UNITS)
                target = held.at[n, h, rows, :]
                pairs.append((source.at[:, columns], target))
    loads = copy_all(pairs, sems)
    stores = []
    for n in range(4):
        wait_all(loads[4 * n : 4 * n + 4])
        stores += copy_all([(held.at[n], outs[n])], sems, 16 + n)
    wait_all(stores)


def arrange_weights(where, w_gate, w_up):
    return pl.pallas_call(
        arrange_kernel,
        out_shape=[pltpu.HBM((2, 2 * UNITS, 256), BF)] * 4,
        in_specs=[SMEM] + [ANY] * 2,
        out_specs=[ANY] * 4,
        scratch_shapes=[
            pltpu.VMEM((4, 2, 2 * UNITS, 256), BF),
            pltpu.SemaphoreType.DMA((20,)),
        ],
        compiler_params=params(8),
        cost_estimate=cost(0, 8_000_000),
        name="arrange_weights",
    )(where, w_gate, w_up)


def part_kernel(chunks, grads, got, own, given, router_a, router_b, *outs):
    tail = hi_lo(router_a[...] + router_b[...])
    for n, (j, out) in enumerate(zip(chunks, outs)):
        total = dot(grads[...], own[n], ((1,), (0,)))
        total = total + dot(got[...], given[n], ((1,), (0,)))
        if j == 0:
            out[...] = total
        else:
            out[:ROWS, :] = total.astype(BF)
            out[ROWS:, :TOK] = tail
            out[ROWS:, TOK:] = jnp.zeros((16, TOK), BF)


def part_work(chunks, grads, got, own, given, router_a, router_b):
    shapes = [
        jax.ShapeDtypeStruct((ROWS, 256), F32)
        if j == 0
        else jax.ShapeDtypeStruct((ROWS + 16, 256), BF)
        for j in chunks
    ]
    return pl.pallas_call(
        functools.partial(part_kernel, chunks),
        out_shape=shapes,
        in_specs=[VMEM] * 6,
        out_specs=[VMEM] * 2,
        compiler_params=params(8),
        cost_estimate=cost(2 * ROWS * 4 * UNITS * 512, 6_000_000),
        name="part_work",
    )(grads, got, own, given, router_a, router_b)


def hi_lo(value):
    high = value.astype(BF)
    return jnp.concatenate([high.astype(F32), value - high.astype(F32)]).astype(BF)


def x_sum_kernel(blocks, where_ref, keep, router_a, router_b, *refs):
    arrived, outs = refs[:3], refs[3:]
    x = where_ref[0]
    own = hi_lo(router_a[...] + router_b[...]).astype(F32)
    tails = [own] + [a[ROWS:, :TOK].astype(F32) for a in arrived]
    tails = [t[:8] + t[8:] for t in tails]
    total = jnp.zeros((8, TOK), F32)
    for at in range(4):
        j = lax.rem(x - at + 4, 4)
        picked = tails[3]
        for k in range(3):
            picked = jnp.where(j == k, tails[k], picked)
        total = total + picked
    tail = hi_lo(total)
    for r, out in zip(blocks, outs):
        rows = slice(r * PAIR, r * PAIR + PAIR)
        block = keep[rows, :]
        for a in arrived:
            block = block + a[rows, :].astype(F32)
        out[:PAIR, :] = block.astype(BF)
        out[PAIR:, :TOK] = tail
        out[PAIR:, TOK:] = jnp.zeros((16, TOK), BF)


def x_sum(blocks, where, keep, router_a, router_b, arrived):
    return pl.pallas_call(
        functools.partial(x_sum_kernel, blocks),
        out_shape=[jax.ShapeDtypeStruct((PAIR + 16, 256), BF)] * len(blocks),
        in_specs=[SMEM] + [VMEM] * 6,
        out_specs=[BLOCK] * len(blocks),
        compiler_params=params(8),
        cost_estimate=cost(1_000_000, 3_000_000),
        name="x_sum",
    )(where, keep, router_a, router_b, *arrived)


def return_kernel(*refs):
    parts, (pack, out_ref) = refs[:4], refs[4:]
    row = lax.broadcasted_iota(jnp.int32, (8, TOK), 0)
    router = jnp.zeros((8, TOK), F32)
    for c in range(2):
        total = jnp.zeros((TOK, 256), F32)
        for r in range(EXPERTS):
            at = (c * EXPERTS + r) * CAP
            hot = pack[at : at + CAP, :]
            total += dot(hot, parts[r][c * CAP : (c + 1) * CAP, :], ((0,), (0,)))
            tail = dot(parts[r][PAIR : PAIR + 16, :CAP], hot, ((1,), (0,)))
            at = 2 * r + c
            value = tail[at : at + 1] + tail[8 + at : 9 + at]
            router = jnp.where(row == 4 * c + r, value, router)
        out_ref[c * TOK : (c + 1) * TOK, :] = total.astype(BF)
    out_ref[2 * TOK :, :TOK] = hi_lo(router)
    out_ref[2 * TOK :, TOK:] = jnp.zeros((16, TOK), BF)


def return_slots(parts, pack):
    return pl.pallas_call(
        return_kernel,
        out_shape=jax.ShapeDtypeStruct((2 * TOK + 16, 256), BF),
        in_specs=[BLOCK] * 5,
        out_specs=BLOCK,
        compiler_params=params(8),
        cost_estimate=cost(100_000_000, 1_500_000),
        name="return_slots",
    )(*parts, pack)


def final_kernel(where_ref, partial, got, pack, stays, goes, router):
    core = where_ref[1]
    total = partial[...].astype(F32) + got[...].astype(F32)
    final = []
    for c in range(2):
        for h in range(2):
            at = HOT + (2 * c + h) * TOK
            columns = slice(h * TOK, h * TOK + TOK)
            rows = total[c * TOK : (c + 1) * TOK, columns]
            final.append(rows + pack[at : at + TOK, :].astype(F32))
    for h in range(2):
        columns = slice(h * TOK, h * TOK + TOK)
        stays[:, columns] = jnp.where(core == 0, final[h], final[2 + h]).astype(BF)
        goes[:, columns] = jnp.where(core == 0, final[2 + h], final[h]).astype(BF)
    tail = total[2 * TOK :, :TOK]
    router[...] = tail[:8] + tail[8:]


def finish(where, partial, got, pack):
    return pl.pallas_call(
        final_kernel,
        out_shape=[
            jax.ShapeDtypeStruct((TOK, 256), BF),
            jax.ShapeDtypeStruct((TOK, 256), BF),
            jax.ShapeDtypeStruct((8, TOK), F32),
        ],
        in_specs=[SMEM] + [BLOCK] * 3,
        out_specs=[BLOCK] * 3,
        compiler_params=params(8),
        cost_estimate=cost(1_000_000, 600_000),
        name="finish",
    )(where, partial, got, pack)


def x_gather(own):
    return [own] + [x_shift(own, j) for j in (1, 2, 3)]


def weight_grad(a, b):
    return dot(a, b, ((0,), (0,))).astype(BF)[None]


def pinned(a):
    return pltpu.with_memory_space_constraint(a, pltpu.HBM)


def on_device(layer_input, out_grad, expert_ids, gate_weights, w_gate, w_up, w_down):
    spot = lax.axis_index("expert")
    chip, core = spot // 2, spot % 2
    x = lax.axis_index("dp") % 4
    where = jnp.stack([x, core]).astype(jnp.int32)
    gate_rows, up_rows = pinned(w_gate[0]), pinned(w_up[0])

    relative = (expert_ids - chip) & 3
    picked = relative.T[None] == jnp.arange(EXPERTS, dtype=jnp.int32)[:, None, None]
    named = jnp.sum(picked.astype(F32), axis=1)
    weight = jnp.sum(jnp.where(picked, gate_weights.T.astype(F32)[None], 0.0), axis=1)
    meta = jnp.pad(jnp.concatenate([named, weight]).astype(BF), ((0, 8), (0, 384)))

    def own_columns(half):
        start = x * 512 + half * 256
        a = lax.dynamic_slice(layer_input, (0, start), (TOK, 256))
        b = lax.dynamic_slice(out_grad, (0, start), (TOK, 256))
        return jnp.concatenate([jnp.concatenate([a, b], axis=1), meta], axis=0)

    mine = own_columns(core)
    got = core_swap(own_columns(1 - core))
    filled = fill_slots(where, mine, got)
    gate0, pack = filled[3:]
    away = {r: chip_shift(filled[r - 1], r) for r in (2, 1, 3)}
    away = [away[r] for r in (1, 2, 3)]
    own_a, own_b, give_a, give_b = arrange_weights(where, gate_rows, up_rows)
    local = local_slots(mine, layer_input, out_grad)
    away, given, local = lax.optimization_barrier((away, [give_a, give_b], local))
    local = [local, core_swap(local)]
    rows = [z[:PAIR] for z in away] + [z[PAIR : 2 * PAIR] for z in away]
    pieces = x_gather(jnp.concatenate(rows))
    given = [core_swap(g) for g in given]
    own, near, given, pack = lax.optimization_barrier((pieces[0], pieces[1], given, pack))
    pack = section_shift(pack, -1)
    given = [pinned(g) for g in given]
    pieces[2], pieces[3], pack = lax.optimization_barrier((pieces[2], pieces[3], pack))
    pieces[:2] = own, near
    gates = jnp.stack([gate0[:2, :CAP]] + [z[2 * PAIR : 2 * PAIR + 2, :CAP] for z in away])
    gates = gates.astype(F32).reshape(ROWS, 1)
    pieces = pieces + [core_swap(p) for p in pieces]
    pieces, given = lax.optimization_barrier((pieces, given))

    rows_input, rows_grad, gpg, upg, scaled, router, half = expert_work(
        where, pieces, local, w_gate[0], w_up[0], w_down[0], gates
    )
    got = core_swap(half)
    router = jnp.pad(router.reshape(8, CAP), ((0, 0), (0, TOK - CAP)))
    routers = (router, core_swap(router))
    far, near = part_work(CHUNKS[0], half, got, own_a, given[0], *routers)
    far, near = x_shift(far, 2), x_shift(near, 1)
    back, keep = part_work(CHUNKS[1], half, got, own_b, given[1], *routers)
    gpg, upg, scaled, keep = lax.optimization_barrier((gpg, upg, scaled, keep))
    arrived = [near, far, x_shift(back, 3)]
    grads = [weight_grad(gpg, rows_input), weight_grad(upg, rows_input)]
    keep, grads = lax.optimization_barrier((keep, grads))
    (far_block,) = x_sum((2,), where, keep, *routers, arrived)
    far_block, keep = lax.optimization_barrier((far_block, keep))
    blocks = x_sum((0, 1, 3), where, keep, *routers, arrived)
    blocks, scaled = lax.optimization_barrier((blocks, scaled))
    blocks = {0: blocks[0], 1: blocks[1], 3: blocks[2], 2: far_block}
    blocks = [chip_return(blocks[r], r) for r in range(EXPERTS)]
    grads.append(weight_grad(scaled, rows_grad))
    blocks, grads = lax.optimization_barrier((blocks, grads))

    partial = return_slots(blocks, pack)
    stays, goes, by_expert = finish(where, partial, pair_swap(partial), pack)
    by_expert = section_shift(by_expert, 1)
    goes = core_swap(goes)
    low = jnp.where(core == 0, stays, goes)
    high = jnp.where(core == 0, goes, stays)
    block = jnp.concatenate([low, high], axis=1)
    prev_grad = jnp.zeros((TOK, D), BF)
    pieces = [block] + [x_shift(block, j) for j in (1, 2, 3)]
    for j, piece in enumerate(pieces):
        prev_grad = lax.dynamic_update_slice(prev_grad, piece, (0, (x - j) % 4 * 512))
    by_expert = jnp.where(core == 0, by_expert[:4], by_expert[4:])
    router_grad = jnp.sum(jnp.where(picked, by_expert[:, None, :], 0.0), axis=0).T
    return (prev_grad, router_grad, *grads)


def solution(mesh):
    tokens = P(("section", "expert"), None)
    units = P("section", ("expert", "dp"), None)
    return jax.shard_map(
        on_device,
        mesh=mesh,
        in_specs=(tokens, tokens, tokens, tokens, units, units, units),
        out_specs=(tokens, tokens, units, units, units),
        check_vma=False,
    )
```

```python
import functools

import jax
import jax.numpy as jnp
from jax import lax
from jax.experimental import pallas as pl
from jax.experimental.pallas import tpu as pltpu
from jax.sharding import PartitionSpec as P

EXPERTS = 4
CAP = 80
TOK = 128
D = 2048
UNITS = 512
ROWS = 640
PAIR = 2 * CAP
AWAY = ROWS - PAIR
HOT = 2 * EXPERTS * CAP
BF = jnp.bfloat16
F32 = jnp.float32
MIB = 1 << 20


def cost(flops, moved):
    return pl.CostEstimate(flops=flops, bytes_accessed=moved, transcendentals=0)


def core_swap(a):
    return lax.ppermute(a, "expert", [(i, i ^ 1) for i in range(8)])


def chip_shift(a, r):
    if r != 2:
        return lax.ppermute(a, "expert", [(i, (i + 2 * r) % 8) for i in range(8)])
    route = [(e * 8 + d, (e + 4) % 8 * 8 + (d + 4) % 8) for e in range(8) for d in range(8)]
    return lax.ppermute(a, ("expert", "dp"), route)


def chip_return(a, r):
    route = []
    for s in range(4):
        for e in range(8):
            for d in range(8):
                to = ((s - 1) % 4 * 8 + (e - 2 * r) % 8) * 8 + (d + (4 if r == 2 else 0)) % 8
                route.append(((s * 8 + e) * 8 + d, to))
    return lax.ppermute(a, ("section", "expert", "dp"), route)


def x_shift(a, j):
    return lax.ppermute(a, "dp", [(i, i // 4 * 4 + (i + j) % 4) for i in range(8)])


def pair_swap(a):
    return lax.ppermute(a, "dp", [(i, (i + 4) % 8) for i in range(8)])


def section_shift(a, by):
    return lax.ppermute(a, "section", [(s, (s + by) % 4) for s in range(4)])


def dot(a, b, dims):
    return lax.dot_general(a, b, (dims, ((), ())), preferred_element_type=F32)


def place_rows(meta):
    earlier = lax.broadcasted_iota(jnp.int32, (TOK, TOK), 0)
    later = lax.broadcasted_iota(jnp.int32, (TOK, TOK), 1)
    upto = (earlier <= later).astype(F32).astype(BF)
    return dot(meta, upto, ((1,), (0,))) - 1.0


def hot_rows(named, place, r):
    slot = lax.broadcasted_iota(jnp.int32, (TOK, TOK), 0).astype(F32)
    hit = (slot == place[r : r + 1]) & (named[r : r + 1] > 0.5)
    return hit.astype(F32).astype(BF)


def slots_kernel(where_ref, mine_ref, got_ref, *outs):
    sends, gate0, pack = outs[:3], outs[3], outs[4]
    core = where_ref[1]
    row = lax.broadcasted_iota(jnp.int32, (16, TOK), 0)
    gate_rows = []
    for c in range(2):
        block = jnp.where(core == c, mine_ref[...].astype(F32), got_ref[...].astype(F32)).astype(BF)
        tokens = block[:TOK]
        meta = block[TOK : TOK + 16, :TOK]
        named = meta.astype(F32)
        place = place_rows(meta)
        for h in range(2):
            at = HOT + (2 * c + h) * TOK
            pack[at : at + TOK, :] = tokens[:, 256 + h * TOK : 384 + h * TOK]
        for r in range(EXPERTS):
            hot = hot_rows(named, place, r)
            at = (c * EXPERTS + r) * CAP
            pack[at : at + CAP, :] = hot[:CAP]
            if r > 0:
                filled = dot(hot[:CAP], tokens, ((1,), (0,))).astype(BF)
                sends[r - 1][c * CAP : (c + 1) * CAP, :] = filled[:, :256]
                sends[r - 1][PAIR + c * CAP : PAIR + (c + 1) * CAP, :] = filled[:, 256:]
            gates = dot(meta, hot, ((1,), (1,)))
            gate_rows.append(gates[4 + r : 5 + r])
    for r in range(EXPERTS):
        tile = jnp.where(row == 0, gate_rows[r], jnp.where(row == 1, gate_rows[4 + r], 0.0))
        if r == 0:
            gate0[...] = tile.astype(BF)
        else:
            sends[r - 1][2 * PAIR :, :TOK] = tile.astype(BF)
            sends[r - 1][2 * PAIR :, TOK:] = jnp.zeros((16, TOK), BF)


BLOCK = pl.BlockSpec()
VMEM = pl.BlockSpec(memory_space=pltpu.VMEM)
ANY = pl.BlockSpec(memory_space=pltpu.HBM)
SMEM = pl.BlockSpec(memory_space=pltpu.SMEM)


def params(mib):
    return pltpu.CompilerParams(vmem_limit_bytes=mib * MIB)


def fill_slots(where, mine, got):
    shapes = (
        [jax.ShapeDtypeStruct((2 * PAIR + 16, 256), BF)] * 3
        + [
            jax.ShapeDtypeStruct((16, TOK), BF),
            jax.ShapeDtypeStruct((HOT + 4 * TOK, TOK), BF),
        ]
    )
    return pl.pallas_call(
        slots_kernel,
        out_shape=shapes,
        in_specs=[SMEM] + [BLOCK] * 2,
        out_specs=[BLOCK] * 5,
        compiler_params=params(8),
        cost_estimate=cost(100_000_000, 2_000_000),
        name="fill_slots",
    )(where, mine, got)


def local_kernel(mine_ref, input_ref, grad_ref, out_ref):
    meta = mine_ref[TOK : TOK + 16, :TOK]
    hot = hot_rows(meta.astype(F32), place_rows(meta), 0)[:CAP]
    for at, source in enumerate((input_ref, grad_ref)):
        for part in range(4):
            columns = slice(part * 512, part * 512 + 512)
            out_ref[at, :, columns] = dot(hot, source[:, columns], ((1,), (0,))).astype(BF)


def local_slots(mine, layer_input, out_grad):
    return pl.pallas_call(
        local_kernel,
        out_shape=pltpu.HBM((2, CAP, D), BF),
        in_specs=[BLOCK] * 3,
        out_specs=BLOCK,
        compiler_params=params(8),
        cost_estimate=cost(100_000_000, 2_000_000),
        name="local_slots",
    )(mine, pinned(layer_input), pinned(out_grad))


def column(where_ref, j, flip):
    x, core = where_ref[0], where_ref[1]
    half = core if flip == 0 else 1 - core
    return pl.multiple_of(lax.rem(x + j, 4) * 512 + half * 256, 256)


def copy_all(pairs, sems, first=0):
    copies = [
        pltpu.make_async_copy(source, target, sems.at[first + at])
        for at, (source, target) in enumerate(pairs)
    ]
    for c in copies:
        c.start()
    return copies


def wait_all(copies):
    for c in copies:
        c.wait()


def gather_rows(where_ref, pieces, local, which, whole):
    core = where_ref[1]
    pairs = []
    for flip in range(2):
        half = core if flip == 0 else 1 - core
        rows = pl.ds(pl.multiple_of(half * CAP, 16), CAP)
        pairs.append((local[flip].at[which], whole.at[rows, :]))
        for j, piece in enumerate(pieces[4 * flip : 4 * flip + 4]):
            columns = pl.ds(column(where_ref, (4 - j) % 4, flip), 256)
            rows = slice(which * AWAY, which * AWAY + AWAY)
            pairs.append((piece.at[rows, :], whole.at[PAIR:, columns]))
    return pairs


def expert_kernel(where_ref, *refs):
    pieces, local = refs[:8], refs[8:10]
    up_hbm, down_hbm, gate_rows, gates_ref = refs[10:14]
    input_out, grad_out, gpg_out, upg_out, scaled_out, router, grads = refs[14:21]
    inputs, out_grads, scaled, up_rows, down_rows, pre_gate, sems = refs[21:]
    wait_all(copy_all(gather_rows(where_ref, pieces, local, 0, inputs), sems))
    loads = copy_all(
        [(up_hbm, up_rows)]
        + gather_rows(where_ref, pieces, local, 1, out_grads)
        + [(down_hbm, down_rows)],
        sems,
        10,
    )
    stores = copy_all([(inputs, input_out)], sems, 22)
    for n in range(2):
        units = slice(n * 256, n * 256 + 256)
        pre_gate[:, units] = dot(inputs[...], gate_rows[units, :], ((1,), (1,)))
    loads[0].wait()
    gates = gates_ref[...]
    router_sum = jnp.zeros((ROWS, 1), F32)
    for n in range(2):
        units = slice(n * 256, n * 256 + 256)
        ups = slice(UNITS + n * 256, UNITS + n * 256 + 256)
        v = pre_gate[:, units]
        up = dot(inputs[...], up_rows[units, :], ((1,), (1,)))
        if n == 0:
            wait_all(loads[1:])
            stores += copy_all([(out_grads, grad_out)], sems, 23)
        hidden_grad = dot(out_grads[...], down_rows[units, :], ((1,), (1,)))
        s = jax.nn.sigmoid(v)
        activated = v * s
        hidden = activated * up
        router_sum = router_sum + jnp.sum(hidden * hidden_grad, axis=1, keepdims=True)
        scaled_grad = gates * hidden_grad
        grads[:, units] = (scaled_grad * up * (s * (1.0 + v * (1.0 - s)))).astype(BF)
        grads[:, ups] = (scaled_grad * activated).astype(BF)
        scaled[:, units] = (gates * hidden).astype(BF)
        stores += copy_all(
            [
                (grads.at[:, units], gpg_out.at[:, units]),
                (grads.at[:, ups], upg_out.at[:, units]),
                (scaled.at[:, units], scaled_out.at[:, units]),
            ],
            sems,
            24 + 3 * n,
        )
    router[...] = router_sum
    wait_all(stores)


def expert_work(where, pieces, local, w_gate, w_up, w_down, gates):
    return pl.pallas_call(
        expert_kernel,
        out_shape=[
            pltpu.HBM((ROWS, D), BF),
            pltpu.HBM((ROWS, D), BF),
            pltpu.HBM((ROWS, UNITS), BF),
            pltpu.HBM((ROWS, UNITS), BF),
            pltpu.HBM((ROWS, UNITS), BF),
            jax.ShapeDtypeStruct((ROWS, 1), F32),
            jax.ShapeDtypeStruct((ROWS, 2 * UNITS), BF),
        ],
        in_specs=[SMEM] + [ANY] * 12 + [VMEM] * 2,
        out_specs=[ANY] * 5 + [VMEM] * 2,
        scratch_shapes=[
            pltpu.VMEM((ROWS, D), BF),
            pltpu.VMEM((ROWS, D), BF),
            pltpu.VMEM((ROWS, UNITS), BF),
            pltpu.VMEM((UNITS, D), BF),
            pltpu.VMEM((UNITS, D), BF),
            pltpu.VMEM((ROWS, UNITS), F32),
            pltpu.SemaphoreType.DMA((30,)),
        ],
        compiler_params=params(20),
        cost_estimate=cost(3 * 2 * ROWS * D * UNITS, 12_000_000),
        name="expert_work",
    )(where, *map(pinned, pieces), *map(pinned, local), w_up, w_down, w_gate, gates)


CHUNKS = ((2, 1), (3, 0))


def arrange_kernel(where_ref, gate_ref, up_ref, *refs):
    outs, (held, sems) = refs[:4], refs[4:]
    pairs = []
    for n in range(4):
        chunks = CHUNKS[n % 2]
        for h, j in enumerate(chunks):
            columns = pl.ds(column(where_ref, j, n // 2), 256)
            for at, source in enumerate((gate_ref, up_ref)):
                rows = slice(at * UNITS, (at + 1) * UNITS)
                target = held.at[n, h, rows, :]
                pairs.append((source.at[:, columns], target))
    loads = copy_all(pairs, sems)
    stores = []
    for n in range(4):
        wait_all(loads[4 * n : 4 * n + 4])
        stores += copy_all([(held.at[n], outs[n])], sems, 16 + n)
    wait_all(stores)


def arrange_weights(where, w_gate, w_up):
    return pl.pallas_call(
        arrange_kernel,
        out_shape=[pltpu.HBM((2, 2 * UNITS, 256), BF)] * 4,
        in_specs=[SMEM] + [ANY] * 2,
        out_specs=[ANY] * 4,
        scratch_shapes=[
            pltpu.VMEM((4, 2, 2 * UNITS, 256), BF),
            pltpu.SemaphoreType.DMA((20,)),
        ],
        compiler_params=params(8),
        cost_estimate=cost(0, 8_000_000),
        name="arrange_weights",
    )(where, w_gate, w_up)


def part_kernel(chunks, grads, got, own, given, router_a, router_b, *outs):
    tail = hi_lo(router_a[...] + router_b[...])
    for n, (j, out) in enumerate(zip(chunks, outs)):
        total = dot(grads[...], own[n], ((1,), (0,)))
        total = total + dot(got[...], given[n], ((1,), (0,)))
        if j == 0:
            out[...] = total
        else:
            out[:ROWS, :] = total.astype(BF)
            out[ROWS:, :TOK] = tail
            out[ROWS:, TOK:] = jnp.zeros((16, TOK), BF)


def part_work(chunks, grads, got, own, given, router_a, router_b):
    shapes = [
        jax.ShapeDtypeStruct((ROWS, 256), F32)
        if j == 0
        else jax.ShapeDtypeStruct((ROWS + 16, 256), BF)
        for j in chunks
    ]
    return pl.pallas_call(
        functools.partial(part_kernel, chunks),
        out_shape=shapes,
        in_specs=[VMEM] * 6,
        out_specs=[VMEM] * 2,
        compiler_params=params(8),
        cost_estimate=cost(2 * ROWS * 4 * UNITS * 512, 6_000_000),
        name="part_work",
    )(grads, got, own, given, router_a, router_b)


def hi_lo(value):
    high = value.astype(BF)
    return jnp.concatenate([high.astype(F32), value - high.astype(F32)]).astype(BF)


def x_sum_kernel(blocks, where_ref, keep, router_a, router_b, *refs):
    arrived, outs = refs[:3], refs[3:]
    x = where_ref[0]
    own = hi_lo(router_a[...] + router_b[...]).astype(F32)
    tails = [own] + [a[ROWS:, :TOK].astype(F32) for a in arrived]
    tails = [t[:8] + t[8:] for t in tails]
    total = jnp.zeros((8, TOK), F32)
    for at in range(4):
        j = lax.rem(x - at + 4, 4)
        picked = tails[3]
        for k in range(3):
            picked = jnp.where(j == k, tails[k], picked)
        total = total + picked
    tail = hi_lo(total)
    for r, out in zip(blocks, outs):
        rows = slice(r * PAIR, r * PAIR + PAIR)
        block = keep[rows, :]
        for a in arrived:
            block = block + a[rows, :].astype(F32)
        out[:PAIR, :] = block.astype(BF)
        out[PAIR:, :TOK] = tail
        out[PAIR:, TOK:] = jnp.zeros((16, TOK), BF)


def x_sum(blocks, where, keep, router_a, router_b, arrived):
    return pl.pallas_call(
        functools.partial(x_sum_kernel, blocks),
        out_shape=[jax.ShapeDtypeStruct((PAIR + 16, 256), BF)] * len(blocks),
        in_specs=[SMEM] + [VMEM] * 6,
        out_specs=[BLOCK] * len(blocks),
        compiler_params=params(8),
        cost_estimate=cost(1_000_000, 3_000_000),
        name="x_sum",
    )(where, keep, router_a, router_b, *arrived)


def return_kernel(*refs):
    parts, (pack, out_ref) = refs[:4], refs[4:]
    row = lax.broadcasted_iota(jnp.int32, (8, TOK), 0)
    router = jnp.zeros((8, TOK), F32)
    for c in range(2):
        total = jnp.zeros((TOK, 256), F32)
        for r in range(EXPERTS):
            at = (c * EXPERTS + r) * CAP
            hot = pack[at : at + CAP, :]
            total += dot(hot, parts[r][c * CAP : (c + 1) * CAP, :], ((0,), (0,)))
            tail = dot(parts[r][PAIR : PAIR + 16, :CAP], hot, ((1,), (0,)))
            at = 2 * r + c
            value = tail[at : at + 1] + tail[8 + at : 9 + at]
            router = jnp.where(row == 4 * c + r, value, router)
        out_ref[c * TOK : (c + 1) * TOK, :] = total.astype(BF)
    out_ref[2 * TOK :, :TOK] = hi_lo(router)
    out_ref[2 * TOK :, TOK:] = jnp.zeros((16, TOK), BF)


def return_slots(parts, pack):
    return pl.pallas_call(
        return_kernel,
        out_shape=jax.ShapeDtypeStruct((2 * TOK + 16, 256), BF),
        in_specs=[BLOCK] * 5,
        out_specs=BLOCK,
        compiler_params=params(8),
        cost_estimate=cost(100_000_000, 1_500_000),
        name="return_slots",
    )(*parts, pack)


def final_kernel(where_ref, partial, got, pack, stays, goes, router):
    core = where_ref[1]
    total = partial[...].astype(F32) + got[...].astype(F32)
    final = []
    for c in range(2):
        for h in range(2):
            at = HOT + (2 * c + h) * TOK
            columns = slice(h * TOK, h * TOK + TOK)
            rows = total[c * TOK : (c + 1) * TOK, columns]
            final.append(rows + pack[at : at + TOK, :].astype(F32))
    for h in range(2):
        columns = slice(h * TOK, h * TOK + TOK)
        stays[:, columns] = jnp.where(core == 0, final[h], final[2 + h]).astype(BF)
        goes[:, columns] = jnp.where(core == 0, final[2 + h], final[h]).astype(BF)
    tail = total[2 * TOK :, :TOK]
    router[...] = tail[:8] + tail[8:]


def finish(where, partial, got, pack):
    return pl.pallas_call(
        final_kernel,
        out_shape=[
            jax.ShapeDtypeStruct((TOK, 256), BF),
            jax.ShapeDtypeStruct((TOK, 256), BF),
            jax.ShapeDtypeStruct((8, TOK), F32),
        ],
        in_specs=[SMEM] + [BLOCK] * 3,
        out_specs=[BLOCK] * 3,
        compiler_params=params(8),
        cost_estimate=cost(1_000_000, 600_000),
        name="finish",
    )(where, partial, got, pack)


def x_gather(own):
    return [own] + [x_shift(own, j) for j in (1, 2, 3)]


def weight_grad(a, b):
    return dot(a, b, ((0,), (0,))).astype(BF)[None]


def pinned(a):
    return pltpu.with_memory_space_constraint(a, pltpu.HBM)


def on_device(layer_input, out_grad, expert_ids, gate_weights, w_gate, w_up, w_down):
    spot = lax.axis_index("expert")
    chip, core = spot // 2, spot % 2
    x = lax.axis_index("dp") % 4
    where = jnp.stack([x, core]).astype(jnp.int32)
    gate_rows, up_rows = pinned(w_gate[0]), pinned(w_up[0])

    relative = (expert_ids - chip) & 3
    picked = relative.T[None] == jnp.arange(EXPERTS, dtype=jnp.int32)[:, None, None]
    named = jnp.sum(picked.astype(F32), axis=1)
    weight = jnp.sum(jnp.where(picked, gate_weights.T.astype(F32)[None], 0.0), axis=1)
    meta = jnp.pad(jnp.concatenate([named, weight]).astype(BF), ((0, 8), (0, 384)))

    def own_columns(half):
        start = x * 512 + half * 256
        a = lax.dynamic_slice(layer_input, (0, start), (TOK, 256))
        b = lax.dynamic_slice(out_grad, (0, start), (TOK, 256))
        return jnp.concatenate([jnp.concatenate([a, b], axis=1), meta], axis=0)

    mine = own_columns(core)
    got = core_swap(own_columns(1 - core))
    filled = fill_slots(where, mine, got)
    gate0, pack = filled[3:]
    away = {r: chip_shift(filled[r - 1], r) for r in (2, 1, 3)}
    away = [away[r] for r in (1, 2, 3)]
    own_a, own_b, give_a, give_b = arrange_weights(where, gate_rows, up_rows)
    local = local_slots(mine, layer_input, out_grad)
    away, given, local = lax.optimization_barrier((away, [give_a, give_b], local))
    local = [local, core_swap(local)]
    rows = [z[:PAIR] for z in away] + [z[PAIR : 2 * PAIR] for z in away]
    pieces = x_gather(jnp.concatenate(rows))
    given = [core_swap(g) for g in given]
    own, near, given, pack = lax.optimization_barrier((pieces[0], pieces[1], given, pack))
    pack = section_shift(pack, -1)
    given = [pinned(g) for g in given]
    pieces[2], pack = lax.optimization_barrier((pieces[2], pack))
    pieces[:2] = own, near
    gates = jnp.stack([gate0[:2, :CAP]] + [z[2 * PAIR : 2 * PAIR + 2, :CAP] for z in away])
    gates = gates.astype(F32).reshape(ROWS, 1)
    pieces = pieces + [core_swap(p) for p in pieces]
    pieces, given = lax.optimization_barrier((pieces, given))

    rows_input, rows_grad, gpg, upg, scaled, router, half = expert_work(
        where, pieces, local, w_gate[0], up_rows, pinned(w_down[0]), gates
    )
    got = core_swap(half)
    router = jnp.pad(router.reshape(8, CAP), ((0, 0), (0, TOK - CAP)))
    routers = (router, core_swap(router))
    far, near = part_work(CHUNKS[0], half, got, own_a, given[0], *routers)
    far, near = x_shift(far, 2), x_shift(near, 1)
    back, keep = part_work(CHUNKS[1], half, got, own_b, given[1], *routers)
    gpg, upg, scaled, keep = lax.optimization_barrier((gpg, upg, scaled, keep))
    arrived = [near, far, x_shift(back, 3)]
    grads = [weight_grad(gpg, rows_input), weight_grad(upg, rows_input)]
    keep, grads = lax.optimization_barrier((keep, grads))
    (far_block,) = x_sum((2,), where, keep, *routers, arrived)
    far_block, keep = lax.optimization_barrier((far_block, keep))
    blocks = x_sum((0, 1, 3), where, keep, *routers, arrived)
    blocks, scaled = lax.optimization_barrier((blocks, scaled))
    blocks = {0: blocks[0], 1: blocks[1], 3: blocks[2], 2: far_block}
    blocks = [chip_return(blocks[r], r) for r in range(EXPERTS)]
    grads.append(weight_grad(scaled, rows_grad))
    blocks, grads = lax.optimization_barrier((blocks, grads))

    partial = return_slots(blocks, pack)
    stays, goes, by_expert = finish(where, partial, pair_swap(partial), pack)
    by_expert = section_shift(by_expert, 1)
    goes = core_swap(goes)
    low = jnp.where(core == 0, stays, goes)
    high = jnp.where(core == 0, goes, stays)
    block = jnp.concatenate([low, high], axis=1)
    prev_grad = jnp.zeros((TOK, D), BF)
    pieces = [block] + [x_shift(block, j) for j in (1, 2, 3)]
    for j, piece in enumerate(pieces):
        prev_grad = lax.dynamic_update_slice(prev_grad, piece, (0, (x - j) % 4 * 512))
    by_expert = jnp.where(core == 0, by_expert[:4], by_expert[4:])
    router_grad = jnp.sum(jnp.where(picked, by_expert[:, None, :], 0.0), axis=0).T
    return (prev_grad, router_grad, *grads)


def solution(mesh):
    tokens = P(("section", "expert"), None)
    units = P("section", ("expert", "dp"), None)
    return jax.shard_map(
        on_device,
        mesh=mesh,
        in_specs=(tokens, tokens, tokens, tokens, units, units, units),
        out_specs=(tokens, tokens, units, units, units),
        check_vma=False,
    )
```
